512 devices in a mesh: dp: 16 (over y, z_hi), head: 32 (over x, z_lo, core).
Axes of the slice: x: 4, y: 4, z: 16 (z_hi: 4, z_lo: 4; z = z_hi * 4 + z_lo), core: 2. Of those that a mesh axis runs over, the one named last changes fastest.
Arguments:
- queries: bfloat16 [16, 768, 12288], P('dp', None, 'head'), may hold values from -6 to 6
- key_rows: bfloat16 [16, 768, 512], P('dp', 'head'), may hold values from -6 to 6
- value_rows: bfloat16 [16, 768, 512], P('dp', 'head'), may hold values from -6 to 6
- upstream: bfloat16 [16, 768, 12288], P('dp', None, 'head'), may hold values from -6 to 6
- head_gate: float32 [192], P('head'), may hold values from 0.5 to 2
- slot_heads: int32 [192], P('head'), may hold values from 0 to 231, as said below
Outputs:
- query_grad: bfloat16 [16, 768, 12288], P('dp', None, 'head')
- key_grad: bfloat16 [16, 768, 512], P('dp', 'head')
- value_grad: bfloat16 [16, 768, 512], P('dp', 'head')
- gate_grad: float32 [192], P('head')
The draws below stay inside these ranges and needn't reach their ends.
Inputs may be any that keep to these rules, and one draw needn't show every extreme that they name: `slot_heads`: distinct initial head numbers in an arbitrary order; slot j of the head index i is entry i * 6 + j.
All inputs are finite; a program needn't handle non-finite values.
Results may differ from the reference program's by a relative error of at most 0.035.
Values may be sent and summed in bfloat16 or wider, within the bound.
A program may use at most 64 MiB of HBM per device.

```python
import math
from functools import partial
import jax
import jax.numpy as jnp
from jax import lax

HEAD_DIM = 64
KV_HEADS = 8
HEADS_ALL = 232
GROUP_HEADS = 29
HEAD_DEV = 6
SEQ = 768
KEPT = 192
BATCH = 16
N_HEAD = 32


def kept_heads(key):
    key = jax.random.fold_in(key, 101)
    first, second = jax.random.split(key)
    inner = 1 + jax.random.permutation(first, HEADS_ALL - 2).astype(jnp.int32)
    chosen = jnp.concatenate([jnp.zeros((1,), jnp.int32), inner[HEADS_ALL - KEPT:], jnp.full((1,), HEADS_ALL - 1, jnp.int32)])
    return chosen[jax.random.permutation(second, KEPT)]


def draw_slot_heads(key, part):
    return kept_heads(key)


def draw_queries(key, part):
    key = jax.random.fold_in(key, 3)
    base = jnp.clip(jax.random.normal(key, (BATCH, SEQ, KEPT, HEAD_DIM)), -6.0, 6.0)
    return base.reshape(BATCH, SEQ, KEPT * HEAD_DIM).astype(jnp.bfloat16)


def draw_key_rows(key, part):
    key = jax.random.fold_in(key, 5)
    base = jnp.clip(jax.random.normal(key, (BATCH, SEQ, KV_HEADS, HEAD_DIM)), -6.0, 6.0)
    return base.reshape(BATCH, SEQ, KV_HEADS * HEAD_DIM).astype(jnp.bfloat16)


def with_spikes(values, own_key, source, target, shards_of, factor):
    def block_of(axis_at):
        return (jnp.arange(values.shape[axis_at]) // (values.shape[axis_at] // shards_of)).reshape((-1,) + (1,) * (values.ndim - 1 - axis_at))

    one_side = jax.random.permutation(own_key, shards_of)[block_of(target)]
    far = (block_of(target) + shards_of // 2) % shards_of
    return jnp.where((block_of(source) == one_side) | (block_of(source) == far), factor * values, values)


def block_levels(own_key, shape, cuts, smallest, high):
    def one(dim, shards_of):
        steps = jax.random.uniform(jax.random.fold_in(jax.random.fold_in(own_key, 6), dim), (shards_of,), jnp.float32, smallest / len(cuts), high / len(cuts))
        return jnp.repeat(jnp.exp(steps), shape[dim] // shards_of).reshape((-1,) + (1,) * (len(shape) - dim - 1))

    factor_of = one(*cuts[0])
    for cut in cuts[1:]:
        factor_of = factor_of * one(*cut)
    return factor_of


def scatter_about(own_key, dims, spread, reach, pieces=(), held_as=jnp.bfloat16):
    gain = block_levels(own_key, dims, pieces, -0.22, 0.18) if pieces else 1.0
    array = jax.random.normal(own_key, dims, jnp.float32) * spread * gain
    return jnp.minimum(jnp.maximum(array, -reach), reach).astype(held_as)


def gaussian_with(key, extent, width, limit, cuts, heavy, held_as=jnp.bfloat16):
    array = width * jax.random.normal(key, extent, jnp.float32)
    if cuts:
        array = array * block_levels(key, extent, cuts, -0.22, 0.18)
    return jnp.clip(with_spikes(array, jax.random.fold_in(key, 3), *heavy), -limit, limit).astype(held_as)


def setup_inputs(seed: int = 0) -> dict:
    streams_of = jax.random.split(jax.random.key(seed), 7)
    queries = draw_queries(jax.random.fold_in(streams_of[6], 71), 0)
    key_rows = draw_key_rows(jax.random.fold_in(streams_of[6], 71), 0)
    value_rows = scatter_about(streams_of[2], (BATCH, SEQ, KV_HEADS * HEAD_DIM), 1.0, 6.0, ((0, 16), (1, 32)))
    upstream = gaussian_with(streams_of[3], (BATCH, SEQ, KEPT * HEAD_DIM), 1.0, 6.0, ((0, 16), (2, 32)), (2, 1, 32, 2.75))
    head_gate = jnp.clip(jnp.exp(math.log(2.0) - 1.3862944 * jax.random.uniform(streams_of[4], (KEPT,), jnp.float32) ** block_levels(streams_of[4], (KEPT,), ((0, 32),), -0.2, 0.2)), 0.5, 2.0)
    slot_heads = draw_slot_heads(jax.random.fold_in(streams_of[6], 71), 0)
    return dict(queries=queries, key_rows=key_rows, value_rows=value_rows, upstream=upstream, head_gate=head_gate, slot_heads=slot_heads)


score_scale = 0.125


def head_backward(q_head, k_head, v_head, dy_head, gate_one):
    length = q_head.shape[0]
    scores = score_scale * jnp.dot(q_head, k_head.T, preferred_element_type=jnp.float32)
    position = jnp.arange(length, dtype=jnp.int32)
    scores = jnp.where(position[:, None] >= position[None, :], scores, -jnp.inf)
    row_max = jnp.max(scores, axis=1, keepdims=True)
    exponent = jnp.exp(scores - row_max)
    row_sum = jnp.sum(exponent, axis=1, keepdims=True)
    weights = exponent / row_sum
    weights_low = weights.astype(jnp.bfloat16)
    attended = jnp.dot(weights_low, v_head, preferred_element_type=jnp.float32)
    upstream_wide = dy_head.astype(jnp.float32)
    gate_term = jnp.sum(upstream_wide * attended)
    out_grad = (gate_one * upstream_wide).astype(jnp.bfloat16)
    row_delta = jnp.sum(out_grad.astype(jnp.float32) * attended, axis=1, keepdims=True)
    weight_grad = jnp.dot(out_grad, v_head.T, preferred_element_type=jnp.float32)
    score_grad = (weights * (weight_grad - row_delta)).astype(jnp.bfloat16)
    query_grad = (score_scale * jnp.dot(score_grad, k_head, preferred_element_type=jnp.float32)).astype(jnp.bfloat16)
    key_grad = score_scale * jnp.dot(score_grad.T, q_head, preferred_element_type=jnp.float32)
    value_grad = jnp.dot(weights_low.T, out_grad, preferred_element_type=jnp.float32)
    return query_grad, key_grad, value_grad, gate_term


def sequence_backward(inputs, slot_heads, head_gate):
    queries, key_rows, value_rows, upstream = inputs
    length = queries.shape[0]
    q_heads = queries.reshape(length, KEPT, HEAD_DIM).transpose(1, 0, 2).reshape(N_HEAD, HEAD_DEV, length, HEAD_DIM)
    dy_heads = upstream.reshape(length, KEPT, HEAD_DIM).transpose(1, 0, 2).reshape(N_HEAD, HEAD_DEV, length, HEAD_DIM)
    k_table = key_rows.reshape(length, KV_HEADS, HEAD_DIM)
    v_table = value_rows.reshape(length, KV_HEADS, HEAD_DIM)

    def head_step(running, xs):
        key_sum, value_sum = running
        q_head, dy_head, head_number, gate_one = xs
        group_index = (head_number // GROUP_HEADS).astype(jnp.int32)
        k_head = lax.dynamic_index_in_dim(k_table, group_index, axis=1, keepdims=False)
        v_head = lax.dynamic_index_in_dim(v_table, group_index, axis=1, keepdims=False)
        query_grad, key_grad, value_grad, gate_term = head_backward(q_head, k_head, v_head, dy_head, gate_one)
        key_sum = key_sum.at[:, group_index, :].add(key_grad)
        value_sum = value_sum.at[:, group_index, :].add(value_grad)
        return (key_sum, value_sum), (query_grad, gate_term)

    zero_sums = jnp.zeros((length, KV_HEADS, HEAD_DIM), jnp.float32)

    def device_step(totals, xs):
        key_total, value_total = totals
        parts, outputs = lax.scan(head_step, (zero_sums, zero_sums), xs)
        key_low = lax.optimization_barrier(parts[0].astype(jnp.bfloat16))
        value_low = lax.optimization_barrier(parts[1].astype(jnp.bfloat16))
        return (key_total + key_low.astype(jnp.float32), value_total + value_low.astype(jnp.float32)), outputs

    slot_groups = slot_heads.reshape(N_HEAD, HEAD_DEV)
    gate_groups = head_gate.reshape(N_HEAD, HEAD_DEV)
    sums, outputs = lax.scan(device_step, (zero_sums, zero_sums), (q_heads, dy_heads, slot_groups, gate_groups))
    key_sum, value_sum = sums
    query_grads, gate_terms = outputs
    query_grad = query_grads.reshape(KEPT, length, HEAD_DIM).transpose(1, 0, 2).reshape(length, KEPT * HEAD_DIM)
    key_grad = key_sum.reshape(length, KV_HEADS * HEAD_DIM).astype(jnp.bfloat16)
    value_grad = value_sum.reshape(length, KV_HEADS * HEAD_DIM).astype(jnp.bfloat16)
    return query_grad, key_grad, value_grad, gate_terms.reshape(KEPT)


def reference(queries, key_rows, value_rows, upstream, head_gate, slot_heads):
    results = lax.map(partial(sequence_backward, slot_heads=slot_heads, head_gate=head_gate), (queries, key_rows, value_rows, upstream))
    query_grad, key_grad, value_grad, gate_terms = results
    gate_grad = jnp.sum(gate_terms, axis=0) / BATCH
    return query_grad, key_grad, value_grad, gate_grad
```

```python
import functools

import jax
import jax.numpy as jnp
from jax import lax
from jax.experimental import pallas as pl
from jax.experimental.pallas import tpu as pltpu
from jax.sharding import PartitionSpec as P

HEAD_DIM = 64
KV_HEADS = 8
GROUP_HEADS = 29
SEQ = 768
HEADS = 6
PAIRS = 3
BLK = 256
NBLK = SEQ // BLK
KV_COLS = KV_HEADS * HEAD_DIM
Q_COLS = HEADS * HEAD_DIM
OWN = 24
CHIP = 48
XROWS = 192
SCALE = 0.125
SCALE_LOG2 = 0.125 * 1.4426950408889634
NEG = -1e30
MESH = pl.DeviceIdType.MESH
F32 = jnp.float32
BF16 = jnp.bfloat16


def dot(a, b):
    return lax.dot_general(a, b, (((1,), (0,)), ((), ())), preferred_element_type=F32)


def dot_t(a, b):
    return lax.dot_general(a, b, (((1,), (1,)), ((), ())), preferred_element_type=F32)


def fold(values, op):
    rows, cols = values.shape
    return op(values.reshape(rows // 8, 8, cols), axis=0)


def pack_rows(k, v):
    return jnp.concatenate([k[0:16], v[0:16], k[16:24], v[16:24]], axis=0)


def unpack_rows(block):
    k = jnp.concatenate([block[0:16], block[32:40]], axis=0)
    v = jnp.concatenate([block[16:32], block[40:48]], axis=0)
    return k, v


def kernel(
    slots, gates, q_hbm, dy_hbm, key_ref, value_ref,
    dq_hbm, dk_ref, dv_ref, gg_ref,
    shards, k_all, v_all, sel_t, k_sel, v_sel, k_sel_t, q_ref, dy_ref, dyg_ref, dq_ref,
    s_ref, dp_ref, p_ref, ds_ref, gate_acc, gate_recv,
    part, part_recv, chip_sum, x_recv, x_sum, z_recv,
    load_sem, store_sem, ag_recv, ag_z, ag_x, ag_c,
    c_send, c_recv, x_send, x_recv_sem, z_send, z_recv_sem, g_send, g_recv,
):
    me = lax.axis_index("head")
    x, z, c = me // 8, (me // 2) % 4, me % 2
    dp = lax.axis_index("dp")
    y, zh = dp // 4, dp % 4

    def head_id(xx, zz, cc):
        return {"head": (xx * 4 + zz) * 2 + cc}

    def dp_id(yy, hh):
        return {"dp": yy * 4 + hh}

    partners = (
        [head_id((x + d) % 4, z, c) for d in (1, 2, 3)]
        + [head_id(x, (z + d) % 4, c) for d in (1, 2, 3)]
        + [head_id(x, z, 1 - c)]
        + [dp_id((y + d) % 4, zh) for d in (1, 2, 3)]
        + [dp_id(y, (zh + d) % 4) for d in (1, 2, 3)]
    )
    barrier = pltpu.get_barrier_semaphore()
    for partner in partners:
        pl.semaphore_signal(barrier, inc=1, device_id=partner, device_id_type=MESH)

    loads = []
    for p in range(PAIRS):
        cols = pl.ds(p * 128, 128)
        loads.append(pltpu.make_async_copy(q_hbm.at[0, :, cols], q_ref.at[p], load_sem.at[0, p]))
        loads.append(pltpu.make_async_copy(dy_hbm.at[0, :, cols], dy_ref.at[p], load_sem.at[1, p]))
    for load in loads:
        load.start()

    shards[x, z, c] = pack_rows(
        key_ref[0].astype(F32), value_ref[0].astype(F32)
    ).astype(BF16)

    pl.semaphore_wait(barrier, len(partners))

    def shard_copy(xx, zz, cc, send_sem, target):
        return pltpu.make_async_remote_copy(
            src_ref=shards.at[xx, zz, cc], dst_ref=shards.at[xx, zz, cc],
            send_sem=send_sem, recv_sem=ag_recv.at[xx, zz, cc],
            device_id=target, device_id_type=MESH,
        )

    sends = []

    def send(copy):
        copy.start()
        sends.append(copy)

    def arrived(xx, zz, cc):
        shard_copy(xx, zz, cc, ag_z.at[0], head_id(x, z, 1 - c)).wait_recv()

    for d in (1, 2, 3):
        send(shard_copy(x, z, c, ag_z.at[d - 1], head_id(x, (z + d) % 4, c)))
    for dz in range(4):
        zz = (z + dz) % 4
        if dz:
            arrived(x, zz, c)
        for d in (1, 3, 2):
            send(shard_copy(x, zz, c, ag_x.at[dz, d - 1], head_id((x + d) % 4, z, c)))
        send(shard_copy(x, zz, c, ag_c.at[0, dz], head_id(x, z, 1 - c)))
    for d in (1, 3, 2):
        for dz in range(4):
            xx, zz = (x + d) % 4, (z + dz) % 4
            arrived(xx, zz, c)
            send(shard_copy(xx, zz, c, ag_c.at[d, dz], head_id(x, z, 1 - c)))

    row = lax.broadcasted_iota(jnp.int32, (Q_COLS, KV_COLS), 0)
    col = lax.broadcasted_iota(jnp.int32, (Q_COLS, KV_COLS), 1)
    slot_of_row = row // HEAD_DIM
    group_of_row = jnp.zeros((Q_COLS, KV_COLS), jnp.int32)
    for h in range(HEADS):
        group_of_row = jnp.where(slot_of_row == h, slots[h] // GROUP_HEADS, group_of_row)
    wanted = group_of_row * HEAD_DIM + row % HEAD_DIM
    sel_t[...] = jnp.where(col == wanted, 1.0, 0.0).astype(BF16)

    for load in loads:
        load.wait()
    lane = lax.broadcasted_iota(jnp.int32, (1, 128), 1)
    low_half = lane < HEAD_DIM
    for p in range(PAIRS):
        gate = jnp.where(low_half, gates[2 * p], gates[2 * p + 1])
        dyg_ref[p] = (dy_ref[p].astype(F32) * gate).astype(BF16)

    def unpack_x(xx):
        for zz in range(4):
            rows = pl.ds(XROWS * xx + CHIP * zz, CHIP)
            k0, v0 = unpack_rows(shards[xx, zz, 0].astype(F32))
            k1, v1 = unpack_rows(shards[xx, zz, 1].astype(F32))
            k_all[rows, :] = jnp.concatenate([k0, k1], axis=0).astype(BF16)
            v_all[rows, :] = jnp.concatenate([v0, v1], axis=0).astype(BF16)

    def select_block(j):
        rows = pl.ds(BLK * j, BLK)
        keys, values, chosen = k_all[rows, :], v_all[rows, :], sel_t[...]
        k_block = dot_t(keys, chosen).astype(BF16)
        v_block = dot_t(values, chosen).astype(BF16)
        for p in range(PAIRS):
            k_sel[p, rows, :] = k_block[:, p * 128 : (p + 1) * 128]
            v_sel[p, rows, :] = v_block[:, p * 128 : (p + 1) * 128]
        k_t = dot_t(chosen, keys).astype(BF16)
        for p in range(PAIRS):
            k_sel_t[p, :, rows] = k_t[p * 128 : (p + 1) * 128, :]

    key_pos = lax.broadcasted_iota(jnp.int32, (BLK, BLK), 0)
    query_pos = lax.broadcasted_iota(jnp.int32, (BLK, BLK), 1)
    causal = key_pos <= query_pos
    half_masks = (low_half, jnp.logical_not(low_half))

    def forward_block(i):
        queries = pl.ds(BLK * i, BLK)

        def pair_step(p, carry):
            dq_t = []
            for half in range(2):
                mask = half_masks[half]
                h = 2 * p + half
                q_half = jnp.where(mask, q_ref[p, queries, :], jnp.zeros((), BF16))
                dy_half = jnp.where(mask, dyg_ref[p, queries, :], jnp.zeros((), BF16))
                top = jnp.full((8, BLK), NEG, F32)
                for j in range(i + 1):
                    keys = pl.ds(BLK * j, BLK)
                    s = dot_t(k_sel[p, keys, :], q_half)
                    if j == i:
                        s = jnp.where(causal, s, NEG)
                    top = jnp.maximum(top, fold(s, jnp.max))
                    s_ref[half, keys, :] = s
                    dp_ref[half, keys, :] = dot_t(v_sel[p, keys, :], dy_half)
                top = jnp.max(top, axis=0, keepdims=True) * SCALE_LOG2
                total = jnp.zeros((8, BLK), F32)
                weighted = jnp.zeros((8, BLK), F32)
                step = 64
                for k0 in range(0, BLK * (i + 1), step):
                    keys = pl.ds(k0, step)
                    e = jnp.exp2(s_ref[half, keys, :] * SCALE_LOG2 - top)
                    s_ref[half, keys, :] = e
                    total = total + fold(e, jnp.sum)
                    weighted = weighted + fold(e * dp_ref[half, keys, :], jnp.sum)
                inverse = 1.0 / jnp.sum(total, axis=0, keepdims=True)
                delta = jnp.sum(weighted, axis=0, keepdims=True) * inverse
                for k0 in range(0, BLK * (i + 1), step):
                    keys = pl.ds(k0, step)
                    w = s_ref[half, keys, :] * inverse
                    p_ref[h, keys, queries] = w.astype(BF16)
                    ds_ref[h, keys, queries] = (w * (dp_ref[half, keys, :] - delta)).astype(BF16)
                depth = BLK * (i + 1)
                dq_t.append(
                    SCALE * dot(
                        k_sel_t[p, half * 64 : (half + 1) * 64, 0:depth],
                        ds_ref[h, 0:depth, queries],
                    )
                )
                gate_fold = delta[:, 0:128] + delta[:, 128:256]
                if i == 0:
                    gate_acc[0, pl.ds(h, 1), :] = gate_fold
                else:
                    gate_acc[0, pl.ds(h, 1), :] = gate_acc[0, pl.ds(h, 1), :] + gate_fold
            dq_ref[p, queries, :] = jnp.concatenate(dq_t, axis=0).T.astype(BF16)
            return carry

        lax.fori_loop(0, PAIRS, pair_step, 0)

    stores = []

    def store_queries(i):
        for p in range(PAIRS):
            copy = pltpu.make_async_copy(
                dq_ref.at[p, pl.ds(BLK * i, BLK), :],
                dq_hbm.at[0, pl.ds(BLK * i, BLK), pl.ds(128 * p, 128)],
                store_sem.at[i, p],
            )
            copy.start()
            stores.append(copy)

    gate_acc[0] = jnp.zeros((8, 128), F32)
    ready = ((0, 1), (2,), (3,))
    for i in range(NBLK):
        for xx in ready[i]:
            for zz in range(4):
                arrived(xx, zz, 1 - c)
            unpack_x(xx)
        select_block(i)
        forward_block(i)
        store_queries(i)

    def gate_copy(stage, d, target):
        return pltpu.make_async_remote_copy(
            src_ref=gate_acc.at[stage], dst_ref=gate_recv.at[stage, d - 1],
            send_sem=g_send.at[stage, d - 1], recv_sem=g_recv.at[stage, d - 1],
            device_id=target, device_id_type=MESH,
        )

    for d in (1, 2, 3):
        send(gate_copy(0, d, dp_id((y + d) % 4, zh)))

    def split(lo, hi):
        cuts = sorted({lo, hi} | {b for b in range(0, SEQ, BLK) if lo < b < hi})
        return list(zip(cuts[:-1], cuts[1:]))

    def head_grads(weights_ref, other_ref, lo, hi):
        pieces = []
        for a, b in split(lo, hi):
            start = (a // BLK) * BLK
            row_parts = []
            for p in range(PAIRS):
                even = dot(weights_ref[2 * p, a:b, start:SEQ], other_ref[p, start:SEQ, :])
                odd = dot(weights_ref[2 * p + 1, a:b, start:SEQ], other_ref[p, start:SEQ, :])
                row_parts.append(jnp.where(low_half, even, odd))
            pieces.append(jnp.concatenate(row_parts, axis=1))
        return jnp.concatenate(pieces, axis=0)

    def chip_copy(xx):
        return pltpu.make_async_remote_copy(
            src_ref=part.at[xx, 1 - c], dst_ref=part_recv.at[xx],
            send_sem=c_send.at[xx], recv_sem=c_recv.at[xx],
            device_id=head_id(x, z, 1 - c), device_id_type=MESH,
        )

    def x_copy(xx):
        return pltpu.make_async_remote_copy(
            src_ref=chip_sum.at[xx], dst_ref=x_recv.at[x],
            send_sem=x_send.at[xx], recv_sem=x_recv_sem.at[x],
            device_id=head_id(xx, z, c), device_id_type=MESH,
        )

    def key_block(xx):
        lo, hi = XROWS * xx, XROWS * (xx + 1)
        dk = (SCALE * head_grads(ds_ref, q_ref, lo, hi)).astype(BF16)
        dv = head_grads(p_ref, dyg_ref, lo, hi).astype(BF16)
        dk = dot(dk, sel_t[...])
        dv = dot(dv, sel_t[...])
        for zz in range(4):
            for cc in range(2):
                at = CHIP * zz + OWN * cc
                part[xx, cc, zz] = pack_rows(dk[at : at + OWN], dv[at : at + OWN]).astype(BF16)
        send(chip_copy(xx))

    def chip_add(xx):
        chip_copy(xx).wait_recv()
        for zz in range(4):
            chip_sum[xx, zz] = (
                part[xx, c, zz].astype(F32) + part_recv[xx, zz].astype(F32)
            ).astype(BF16)

        @pl.when(xx != x)
        def _():
            x_copy(xx).start()

    for xx in range(4):
        key_block(xx)
        if xx:
            chip_add(xx - 1)
    chip_add(3)

    gate_sum = gate_acc[0]
    for d in (1, 2, 3):
        gate_copy(0, d, dp_id(y, zh)).wait_recv()
        gate_sum = gate_sum + gate_recv[0, d - 1]
    gate_acc[1] = gate_sum
    for d in (1, 2, 3):
        send(gate_copy(1, d, dp_id(y, (zh + d) % 4)))

    for d in (1, 3, 2):
        src = (x + d) % 4
        pltpu.make_async_remote_copy(
            src_ref=chip_sum.at[src], dst_ref=x_recv.at[src],
            send_sem=x_send.at[src], recv_sem=x_recv_sem.at[src],
            device_id=head_id(src, z, c), device_id_type=MESH,
        ).wait_recv()

    def z_copy(d):
        zz = (z + d) % 4
        return pltpu.make_async_remote_copy(
            src_ref=x_sum.at[zz], dst_ref=z_recv.at[d - 1],
            send_sem=z_send.at[d - 1], recv_sem=z_recv_sem.at[d - 1],
            device_id=head_id(x, zz, c), device_id_type=MESH,
        )

    own = None
    for d in (1, 2, 3, 0):
        zz = (z + d) % 4
        total = chip_sum[x, zz].astype(F32)
        for dx in (1, 2, 3):
            total = total + x_recv[(x + dx) % 4, zz].astype(F32)
        if d:
            x_sum[zz] = total.astype(BF16)
            send(z_copy(d))
        else:
            own = total
    gate_sum = gate_acc[1]
    for d in (1, 2, 3):
        gate_copy(1, d, dp_id(y, zh)).wait_recv()
        gate_sum = gate_sum + gate_recv[1, d - 1]
    for h in range(HEADS):
        gg_ref[h] = jnp.sum(gate_sum[h : h + 1, :]) / (16.0 * gates[h])
    for d in (1, 2, 3):
        z_copy(d).wait_recv()
        own = own + z_recv[d - 1].astype(F32)
    dk, dv = unpack_rows(own)
    dk_ref[0] = dk.astype(BF16)
    dv_ref[0] = dv.astype(BF16)

    for d in (1, 2, 3):
        x_copy((x + d) % 4).wait_send()
    for copy in sends:
        copy.wait_send()
    for copy in stores:
        copy.wait()


def local(queries, key_rows, value_rows, upstream, head_gate, slot_heads):
    vmem = pl.BlockSpec(memory_space=pltpu.VMEM)
    smem = pl.BlockSpec(memory_space=pltpu.SMEM)
    hbm = pl.BlockSpec(memory_space=pl.ANY)
    dma = pltpu.SemaphoreType.DMA
    return pl.pallas_call(
        kernel,
        out_shape=(
            jax.ShapeDtypeStruct(queries.shape, BF16),
            jax.ShapeDtypeStruct(key_rows.shape, BF16),
            jax.ShapeDtypeStruct(value_rows.shape, BF16),
            jax.ShapeDtypeStruct(head_gate.shape, F32),
        ),
        in_specs=[smem, smem, hbm, hbm, vmem, vmem],
        out_specs=(hbm, vmem, vmem, smem),
        scratch_shapes=[
            pltpu.VMEM((4, 4, 2, CHIP, KV_COLS), BF16),
            pltpu.VMEM((SEQ, KV_COLS), BF16),
            pltpu.VMEM((SEQ, KV_COLS), BF16),
            pltpu.VMEM((Q_COLS, KV_COLS), BF16),
            pltpu.VMEM((PAIRS, SEQ, 128), BF16),
            pltpu.VMEM((PAIRS, SEQ, 128), BF16),
            pltpu.VMEM((PAIRS, 128, SEQ), BF16),
            pltpu.VMEM((PAIRS, SEQ, 128), BF16),
            pltpu.VMEM((PAIRS, SEQ, 128), BF16),
            pltpu.VMEM((PAIRS, SEQ, 128), BF16),
            pltpu.VMEM((PAIRS, SEQ, 128), BF16),
            pltpu.VMEM((2, SEQ, BLK), F32),
            pltpu.VMEM((2, SEQ, BLK), F32),
            pltpu.VMEM((HEADS, SEQ, SEQ), BF16),
            pltpu.VMEM((HEADS, SEQ, SEQ), BF16),
            pltpu.VMEM((2, 8, 128), F32),
            pltpu.VMEM((2, 3, 8, 128), F32),
            pltpu.VMEM((4, 2, 4, CHIP, KV_COLS), BF16),
            pltpu.VMEM((4, 4, CHIP, KV_COLS), BF16),
            pltpu.VMEM((4, 4, CHIP, KV_COLS), BF16),
            pltpu.VMEM((4, 4, CHIP, KV_COLS), BF16),
            pltpu.VMEM((4, CHIP, KV_COLS), BF16),
            pltpu.VMEM((3, CHIP, KV_COLS), BF16),
            dma((2, PAIRS)), dma((NBLK, PAIRS)),
            dma((4, 4, 2)), dma((3,)), dma((4, 3)), dma((4, 4)),
            dma((4,)), dma((4,)), dma((4,)), dma((4,)), dma((3,)), dma((3,)),
            dma((2, 3)), dma((2, 3)),
        ],
        compiler_params=pltpu.CompilerParams(
            collective_id=0, has_side_effects=True, vmem_limit_bytes=56 * 1024 * 1024
        ),
        name="attention_backward",
    )(slot_heads, head_gate, queries, upstream, key_rows, value_rows)


def solution(mesh):
    in_specs = (
        P("dp", None, "head"),
        P("dp", "head", None),
        P("dp", "head", None),
        P("dp", None, "head"),
        P("head"),
        P("head"),
    )
    out_specs = (P("dp", None, "head"), P("dp", "head", None), P("dp", "head", None), P("head"))
    return jax.shard_map(local, mesh=mesh, in_specs=in_specs, out_specs=out_specs, check_vma=False)
```

```python
import functools

import jax
import jax.numpy as jnp
from jax import lax
from jax.experimental import pallas as pl
from jax.experimental.pallas import tpu as pltpu
from jax.sharding import PartitionSpec as P

HEAD_DIM = 64
KV_HEADS = 8
GROUP_HEADS = 29
SEQ = 768
HEADS = 6
PAIRS = 3
BLK = 256
NBLK = SEQ // BLK
KV_COLS = KV_HEADS * HEAD_DIM
Q_COLS = HEADS * HEAD_DIM
OWN = 24
CHIP = 48
XROWS = 192
SCALE = 0.125
SCALE_LOG2 = 0.125 * 1.4426950408889634
NEG = -1e30
MESH = pl.DeviceIdType.MESH
F32 = jnp.float32
BF16 = jnp.bfloat16


def dot(a, b):
    return lax.dot_general(a, b, (((1,), (0,)), ((), ())), preferred_element_type=F32)


def dot_t(a, b):
    return lax.dot_general(a, b, (((1,), (1,)), ((), ())), preferred_element_type=F32)


def fold(values, op):
    rows, cols = values.shape
    return op(values.reshape(rows // 8, 8, cols), axis=0)


def pack_rows(rows):
    return jnp.concatenate([rows[:, : KV_COLS // 2], rows[:, KV_COLS // 2 :]], axis=0)


def unpack_rows(block):
    return jnp.concatenate([block[0:OWN], block[OWN:CHIP]], axis=1)


KEY, VALUE = 0, 1


def kernel(
    slots, gates, q_hbm, dy_hbm, key_ref, value_ref,
    dq_hbm, dk_ref, dv_ref, gg_ref,
    shards, k_all, sel_t, k_sel, v_sel, k_sel_t, q_ref, dy_ref, dyg_ref, qn_ref, dyn_ref, dq_ref,
    s_ref, p_ref, ds_ref, scale_ref, gate_acc, gate_recv,
    part, part_recv, chip_sum, x_recv, x_sum, z_recv,
    load_sem, store_sem, agz_send, agz_recv, agx_send, agx_recv, agc_send, agc_recv,
    c_send, c_recv, x_send, x_recv_sem, z_send, z_recv_sem, g_send, g_recv, go,
):
    me = lax.axis_index("head")
    x, z, c = me // 8, (me // 2) % 4, me % 2
    dp = lax.axis_index("dp")
    y, zh = dp // 4, dp % 4

    def head_id(xx, zz, cc):
        return {"head": (xx * 4 + zz) * 2 + cc}

    def dp_id(yy, hh):
        return {"dp": yy * 4 + hh}

    sibling = head_id(x, z, 1 - c)
    near = (z + 1 - 2 * (z % 2), 2 - z // 2, 3 - 3 * (z // 2))

    barrier = pltpu.get_barrier_semaphore()

    def greet(target):
        pl.semaphore_signal(barrier, inc=1, device_id=target, device_id_type=MESH)

    for d in (1, 2, 3):
        greet(head_id(x, (z + d) % 4, c))
        greet(head_id((x + d) % 4, z, c))
        greet(dp_id((y + d) % 4, zh))
    greet(sibling)
    for d in (1, 2, 3):
        pl.when((zh + d) % 4 > zh)(lambda d=d: greet(dp_id(y, (zh + d) % 4)))

    loads = []
    for p in range(PAIRS):
        cols = pl.ds(p * 128, 128)
        loads.append(pltpu.make_async_copy(q_hbm.at[0, :, cols], q_ref.at[p], load_sem.at[0, p]))
        loads.append(pltpu.make_async_copy(dy_hbm.at[0, :, cols], dy_ref.at[p], load_sem.at[1, p]))
    for load in loads:
        load.start()

    shards[KEY, x, c, z] = pack_rows(key_ref[0].astype(F32)).astype(BF16)
    shards[VALUE, x, c, z] = pack_rows(value_ref[0].astype(F32)).astype(BF16)

    pl.semaphore_wait(barrier, 10 + zh)

    sends = []

    def send(copy):
        copy.start()
        sends.append(copy)

    def z_shard(t, source, slot, target):
        return pltpu.make_async_remote_copy(
            src_ref=shards.at[t, x, c, source], dst_ref=shards.at[t, x, c, source],
            send_sem=agz_send.at[t, slot], recv_sem=agz_recv.at[t, source],
            device_id=target, device_id_type=MESH,
        )

    def x_shard(t, xx, zz, slot, d, target):
        return pltpu.make_async_remote_copy(
            src_ref=shards.at[t, xx, c, zz], dst_ref=shards.at[t, xx, c, zz],
            send_sem=agx_send.at[t, slot, d - 1], recv_sem=agx_recv.at[t, xx, zz],
            device_id=target, device_id_type=MESH,
        )

    def c_block(t, xx, cc):
        return pltpu.make_async_remote_copy(
            src_ref=shards.at[t, xx, cc], dst_ref=shards.at[t, xx, cc],
            send_sem=agc_send.at[t, xx], recv_sem=agc_recv.at[t, xx],
            device_id=sibling, device_id_type=MESH,
        )

    def send_z(t):
        for slot, zz in enumerate(near):
            send(z_shard(t, z, slot, head_id(x, zz, c)))

    def send_x(t, slot, zz):
        for d in (1, 3, 2):
            send(x_shard(t, x, zz, slot, d, head_id((x + d) % 4, z, c)))

    def forward_z(t):
        for slot, zz in enumerate(near):
            z_shard(t, zz, slot, sibling).wait_recv()
            send_x(t, slot + 1, zz)
        send(c_block(t, x, c))

    def forward_x(t):
        for d in (1, 3, 2):
            xx = (x + d) % 4
            for zz in (z,) + near:
                x_shard(t, xx, zz, 0, d, sibling).wait_recv()
            send(c_block(t, xx, c))

    send_z(KEY)
    send_x(KEY, 0, z)
    send_z(VALUE)
    forward_z(KEY)
    send_x(VALUE, 0, z)
    forward_z(VALUE)

    for d in (1, 2, 3):
        pl.when((zh + d) % 4 < zh)(
            lambda d=d: pl.semaphore_signal(
                go.at[3 - d], inc=1, device_id=dp_id(y, (zh + d) % 4), device_id_type=MESH
            )
        )

    row = lax.broadcasted_iota(jnp.int32, (Q_COLS, KV_COLS), 0)
    col = lax.broadcasted_iota(jnp.int32, (Q_COLS, KV_COLS), 1)
    slot_of_row = row // HEAD_DIM
    group_of_row = jnp.zeros((Q_COLS, KV_COLS), jnp.int32)
    for h in range(HEADS):
        group_of_row = jnp.where(slot_of_row == h, slots[h] // GROUP_HEADS, group_of_row)
    wanted = group_of_row * HEAD_DIM + row % HEAD_DIM
    sel_t[...] = jnp.where(col == wanted, 1.0, 0.0).astype(BF16)

    for load in loads:
        load.wait()
    low_half = lax.broadcasted_iota(jnp.int32, (1, 128), 1) < HEAD_DIM
    half_masks = (low_half, jnp.logical_not(low_half))
    for p in range(PAIRS):
        gate = jnp.where(low_half, gates[2 * p], gates[2 * p + 1])
        dyg_ref[p] = (dy_ref[p].astype(F32) * gate).astype(BF16)

    def select_x(t, xx):
        c_block(t, xx, 1 - c).wait_recv()
        blocks = []
        for zz in range(4):
            for cc in range(2):
                blocks.append(unpack_rows(shards[t, xx, cc, zz].astype(F32)))
        table = jnp.concatenate(blocks, axis=0).astype(BF16)
        rows = pl.ds(pl.multiple_of(XROWS * xx, XROWS), XROWS)
        if t == KEY:
            k_all[rows, :] = table
        chosen = dot_t(table, sel_t[...]).astype(BF16)
        target = k_sel if t == KEY else v_sel
        for p in range(PAIRS):
            target[p, rows, :] = chosen[:, p * 128 : (p + 1) * 128]

    forward_x(KEY)
    for d in (0, 1, 3, 2):
        select_x(KEY, (x + d) % 4)

    key_pos = lax.broadcasted_iota(jnp.int32, (BLK, BLK), 0)
    query_pos = lax.broadcasted_iota(jnp.int32, (BLK, BLK), 1)
    causal = key_pos <= query_pos
    STEP = 64

    def score_max(i, p, half):
        queries = pl.ds(BLK * i, BLK)
        q_half = jnp.where(half_masks[half], q_ref[p, queries, :], jnp.zeros((), BF16))
        top = jnp.full((8, BLK), NEG, F32)
        for j in range(i + 1):
            keys = pl.ds(BLK * j, BLK)
            s = dot_t(k_sel[p, keys, :], q_half)
            if j == i:
                s = jnp.where(causal, s, NEG)
            top = jnp.maximum(top, fold(s, jnp.max))
            s_ref[half, keys, :] = s
        return jnp.max(top, axis=0, keepdims=True) * SCALE_LOG2

    def exp_block(i, p, half, top):
        queries = pl.ds(BLK * i, BLK)
        h = 2 * p + half
        total = jnp.zeros((8, BLK), F32)
        for k0 in range(0, BLK * (i + 1), STEP):
            keys = pl.ds(k0, STEP)
            e = jnp.exp2(s_ref[half, keys, :] * SCALE_LOG2 - top)
            total = total + fold(e, jnp.sum)
            p_ref[h, keys, queries] = e.astype(BF16)
        inverse = 1.0 / jnp.sum(total, axis=0, keepdims=True)
        scale_ref[h, :, queries] = jnp.broadcast_to(inverse, (8, BLK))
        return jnp.broadcast_to(inverse, (HEAD_DIM, BLK))

    def score_block(i):
        queries = pl.ds(BLK * i, BLK)
        for p in range(PAIRS):
            tops = [score_max(i, p, half) for half in range(2)]
            scales = [exp_block(i, p, half, tops[half]) for half in range(2)]
            scale = jnp.concatenate(scales, axis=0).T
            dyn_ref[p, queries, :] = (dyg_ref[p, queries, :].astype(F32) * scale).astype(BF16)
            qn_ref[p, queries, :] = (q_ref[p, queries, :].astype(F32) * (scale * SCALE)).astype(BF16)

    def weight_grad(i, p, half):
        queries = pl.ds(BLK * i, BLK)
        h = 2 * p + half
        dy_half = jnp.where(half_masks[half], dyg_ref[p, queries, :], jnp.zeros((), BF16))
        weighted = jnp.zeros((8, BLK), F32)
        for j in range(i + 1):
            keys = pl.ds(BLK * j, BLK)
            dp = dot_t(v_sel[p, keys, :], dy_half)
            s_ref[half, keys, :] = dp
            weighted = weighted + fold(p_ref[h, keys, queries].astype(F32) * dp, jnp.sum)
        delta = jnp.sum(weighted, axis=0, keepdims=True) * scale_ref[h, 0:1, queries]
        gate_acc[0, h : h + 1, :] = (
            gate_acc[0, h : h + 1, :] + delta[:, 0:128] + delta[:, 128:256]
        )
        return delta

    def score_grad(i, p, half, delta):
        queries = pl.ds(BLK * i, BLK)
        h = 2 * p + half
        depth = BLK * (i + 1)
        for k0 in range(0, depth, STEP):
            keys = pl.ds(k0, STEP)
            ds_ref[h, keys, queries] = (
                p_ref[h, keys, queries].astype(F32) * (s_ref[half, keys, :] - delta)
            ).astype(BF16)

    def query_grad_t(i, p, half):
        queries = pl.ds(BLK * i, BLK)
        h = 2 * p + half
        depth = BLK * (i + 1)
        return (SCALE * scale_ref[h, 0:1, queries]) * dot(
            k_sel_t[p, half * 64 : (half + 1) * 64, 0:depth], ds_ref[h, 0:depth, queries]
        )

    def grad_block(i):
        queries = pl.ds(BLK * i, BLK)
        for p in range(PAIRS):
            deltas = [weight_grad(i, p, half) for half in range(2)]
            for half in range(2):
                score_grad(i, p, half, deltas[half])
            dq_t = [query_grad_t(i, p, half) for half in range(2)]
            dq_ref[p, queries, :] = jnp.concatenate(dq_t, axis=0).T.astype(BF16)

    stores = []

    def store_queries(i):
        for p in range(PAIRS):
            copy = pltpu.make_async_copy(
                dq_ref.at[p, pl.ds(BLK * i, BLK), :],
                dq_hbm.at[0, pl.ds(BLK * i, BLK), pl.ds(128 * p, 128)],
                store_sem.at[i, p],
            )
            copy.start()
            stores.append(copy)

    def split(lo, hi):
        cuts = sorted({lo, hi} | {b for b in range(0, SEQ, BLK) if lo < b < hi})
        return list(zip(cuts[:-1], cuts[1:]))

    def head_grads(weights_ref, other_ref, lo, hi):
        pieces = []
        for a, b in split(lo, hi):
            start = (a // BLK) * BLK
            row_parts = []
            for p in range(PAIRS):
                even = dot(weights_ref[2 * p, a:b, start:SEQ], other_ref[p, start:SEQ, :])
                odd = dot(weights_ref[2 * p + 1, a:b, start:SEQ], other_ref[p, start:SEQ, :])
                row_parts.append(jnp.where(low_half, even, odd))
            pieces.append(jnp.concatenate(row_parts, axis=1))
        return jnp.concatenate(pieces, axis=0)

    def chip_copy(t, xx):
        return pltpu.make_async_remote_copy(
            src_ref=part.at[t, xx, 1 - c], dst_ref=part_recv.at[t, xx],
            send_sem=c_send.at[t, xx], recv_sem=c_recv.at[t, xx],
            device_id=sibling, device_id_type=MESH,
        )

    def x_copy(t, xx):
        return pltpu.make_async_remote_copy(
            src_ref=chip_sum.at[t, xx], dst_ref=x_recv.at[t, x],
            send_sem=x_send.at[t, xx], recv_sem=x_recv_sem.at[t, x],
            device_id=head_id(xx, z, c), device_id_type=MESH,
        )

    def z_copy(t, slot, zz):
        return pltpu.make_async_remote_copy(
            src_ref=x_sum.at[t, zz], dst_ref=z_recv.at[t, z],
            send_sem=z_send.at[t, slot], recv_sem=z_recv_sem.at[t, z],
            device_id=head_id(x, zz, c), device_id_type=MESH,
        )

    def key_block(t, xx):
        lo, hi = XROWS * xx, XROWS * (xx + 1)
        if t == KEY:
            grads = head_grads(ds_ref, qn_ref, lo, hi)
        else:
            grads = head_grads(p_ref, dyn_ref, lo, hi)
        grads = dot(grads.astype(BF16), sel_t[...])
        for zz in range(4):
            for cc in range(2):
                at = CHIP * zz + OWN * cc
                part[t, xx, cc, zz] = pack_rows(grads[at : at + OWN]).astype(BF16)
        send(chip_copy(t, xx))

    def chip_add(t, xx):
        chip_copy(t, xx).wait_recv()
        for zz in range(4):
            chip_sum[t, xx, zz] = (
                part[t, xx, c, zz].astype(F32) + part_recv[t, xx, zz].astype(F32)
            ).astype(BF16)

        @pl.when(xx != x)
        def _():
            x_copy(t, xx).start()

    def x_add(t):
        for d in (1, 3, 2):
            src = (x + d) % 4
            pltpu.make_async_remote_copy(
                src_ref=chip_sum.at[t, src], dst_ref=x_recv.at[t, src],
                send_sem=x_send.at[t, src], recv_sem=x_recv_sem.at[t, src],
                device_id=head_id(src, z, c), device_id_type=MESH,
            ).wait_recv()
        for slot, zz in enumerate(near + (z,)):
            total = chip_sum[t, x, zz].astype(F32)
            for dx in (1, 2, 3):
                total = total + x_recv[t, (x + dx) % 4, zz].astype(F32)
            x_sum[t, zz] = total.astype(BF16)
            if slot < 3:
                send(z_copy(t, slot, zz))

    def z_add(t, out_ref):
        total = x_sum[t, z].astype(F32)
        for slot, zz in enumerate(near):
            pltpu.make_async_remote_copy(
                src_ref=x_sum.at[t, zz], dst_ref=z_recv.at[t, zz],
                send_sem=z_send.at[t, slot], recv_sem=z_recv_sem.at[t, zz],
                device_id=head_id(x, zz, c), device_id_type=MESH,
            ).wait_recv()
            total = total + z_recv[t, zz].astype(F32)
        out_ref[0] = unpack_rows(total).astype(BF16)

    def gate_copy(stage, d, target):
        return pltpu.make_async_remote_copy(
            src_ref=gate_acc.at[stage], dst_ref=gate_recv.at[stage, d - 1],
            send_sem=g_send.at[stage, d - 1], recv_sem=g_recv.at[stage, d - 1],
            device_id=target, device_id_type=MESH,
        )

    def gate_add(stage):
        total = gate_acc[stage]
        for d in (1, 2, 3):
            gate_copy(stage, d, sibling).wait_recv()
            total = total + gate_recv[stage, d - 1]
        return total

    gate_acc[0] = jnp.zeros((8, 128), F32)

    score_block(2)
    key_block(VALUE, 3)
    score_block(1)
    chip_add(VALUE, 3)
    key_block(VALUE, 2)
    forward_x(VALUE)
    score_block(0)
    chip_add(VALUE, 2)
    key_block(VALUE, 1)
    key_block(VALUE, 0)

    k_sel_t_all = dot_t(sel_t[...], k_all[...]).astype(BF16)
    for p in range(PAIRS):
        k_sel_t[p] = k_sel_t_all[p * 128 : (p + 1) * 128, :]
    for d in (0, 1, 3, 2):
        select_x(VALUE, (x + d) % 4)
    chip_add(VALUE, 1)
    chip_add(VALUE, 0)

    grad_block(2)
    key_block(KEY, 3)
    store_queries(2)
    grad_block(1)
    chip_add(KEY, 3)
    key_block(KEY, 2)
    store_queries(1)
    grad_block(0)
    for d in (1, 2, 3):
        send(gate_copy(0, d, dp_id((y + d) % 4, zh)))
    chip_add(KEY, 2)
    key_block(KEY, 1)
    store_queries(0)
    key_block(KEY, 0)
    chip_add(KEY, 1)
    gate_acc[1] = gate_add(0)
    for d in (1, 2, 3):
        pl.when((zh + d) % 4 > zh)(lambda d=d: pl.semaphore_wait(go.at[d - 1], 1))
    for d in (1, 2, 3):
        send(gate_copy(1, d, dp_id(y, (zh + d) % 4)))
    chip_add(KEY, 0)
    x_add(VALUE)
    z_add(VALUE, dv_ref)
    x_add(KEY)
    z_add(KEY, dk_ref)
    gate_sum = gate_add(1)
    for h in range(HEADS):
        gg_ref[h] = jnp.sum(gate_sum[h : h + 1, :]) / (16.0 * gates[h])

    for t in (KEY, VALUE):
        for d in (1, 2, 3):
            x_copy(t, (x + d) % 4).wait_send()
    for copy in sends:
        copy.wait_send()
    for copy in stores:
        copy.wait()


def finish(*refs):
    ins, outs, held = refs[:4], refs[4:8], refs[8:12]
    sem_in, sem_out = refs[12:]
    parts = [(n, pl.ds(BLK * k, BLK)) for k, n in enumerate((0, 0, 0))] + [(1, None), (2, None), (3, None)]

    def view(ref, rows):
        return ref if rows is None else ref.at[0, rows, :]

    fetch, store = [], []
    for k, (n, rows) in enumerate(parts):
        here = view(held[n], rows)
        fetch.append(pltpu.make_async_copy(view(ins[n], rows), here, sem_in.at[k]))
        store.append(pltpu.make_async_copy(here, view(outs[n], rows), sem_out.at[k]))
    for copy in fetch:
        copy.start()
    for first, second in zip(fetch, store):
        first.wait()
        second.start()
    for copy in store:
        copy.wait()


def local(queries, key_rows, value_rows, upstream, head_gate, slot_heads):
    vmem = pl.BlockSpec(memory_space=pltpu.VMEM)
    smem = pl.BlockSpec(memory_space=pltpu.SMEM)
    hbm = pl.BlockSpec(memory_space=pl.ANY)
    dma = pltpu.SemaphoreType.DMA
    out_shape = (
        jax.ShapeDtypeStruct(queries.shape, BF16),
        jax.ShapeDtypeStruct(key_rows.shape, BF16),
        jax.ShapeDtypeStruct(value_rows.shape, BF16),
        jax.ShapeDtypeStruct(head_gate.shape, F32),
    )
    half = KV_COLS // 2
    rows_of_pair = pltpu.VMEM((PAIRS, SEQ, 128), BF16)
    results = pl.pallas_call(
        kernel,
        out_shape=out_shape,
        in_specs=[smem, smem, hbm, hbm, vmem, vmem],
        out_specs=(hbm, vmem, vmem, smem),
        scratch_shapes=[
            pltpu.VMEM((2, 4, 2, 4, CHIP, half), BF16),
            pltpu.VMEM((SEQ, KV_COLS), BF16),
            pltpu.VMEM((Q_COLS, KV_COLS), BF16),
            rows_of_pair, rows_of_pair,
            pltpu.VMEM((PAIRS, 128, SEQ), BF16),
            rows_of_pair, rows_of_pair, rows_of_pair, rows_of_pair, rows_of_pair, rows_of_pair,
            pltpu.VMEM((2, SEQ, BLK), F32),
            pltpu.VMEM((HEADS, SEQ, SEQ), BF16),
            pltpu.VMEM((HEADS, SEQ, SEQ), BF16),
            pltpu.VMEM((HEADS, 8, SEQ), F32),
            pltpu.VMEM((2, 8, 128), F32),
            pltpu.VMEM((2, 3, 8, 128), F32),
            pltpu.VMEM((2, 4, 2, 4, CHIP, half), BF16),
            pltpu.VMEM((2, 4, 4, CHIP, half), BF16),
            pltpu.VMEM((2, 4, 4, CHIP, half), BF16),
            pltpu.VMEM((2, 4, 4, CHIP, half), BF16),
            pltpu.VMEM((2, 4, CHIP, half), BF16),
            pltpu.VMEM((2, 4, CHIP, half), BF16),
            dma((2, PAIRS)), dma((NBLK, PAIRS)),
            dma((2, 3)), dma((2, 4)), dma((2, 4, 3)), dma((2, 4, 4)), dma((2, 4)), dma((2, 4)),
            dma((2, 4)), dma((2, 4)), dma((2, 4)), dma((2, 4)), dma((2, 3)), dma((2, 4)),
            dma((2, 3)), dma((2, 3)), pltpu.SemaphoreType.REGULAR((3,)),
        ],
        compiler_params=pltpu.CompilerParams(
            collective_id=0, has_side_effects=True, vmem_limit_bytes=58 * 1024 * 1024
        ),
        name="attention_backward",
    )(slot_heads, head_gate, queries, upstream, key_rows, value_rows)
    return pl.pallas_call(
        finish,
        out_shape=out_shape,
        in_specs=[hbm] * 4,
        out_specs=(hbm,) * 4,
        scratch_shapes=[
            pltpu.VMEM(queries.shape, BF16),
            pltpu.VMEM(key_rows.shape, BF16),
            pltpu.VMEM(value_rows.shape, BF16),
            pltpu.SMEM(head_gate.shape, F32),
            dma((6,)), dma((6,)),
        ],
        name="copy_out",
    )(*results)


def solution(mesh):
    in_specs = (
        P("dp", None, "head"),
        P("dp", "head", None),
        P("dp", "head", None),
        P("dp", None, "head"),
        P("head"),
        P("head"),
    )
    out_specs = (P("dp", None, "head"), P("dp", "head", None), P("dp", "head", None), P("head"))
    return jax.shard_map(local, mesh=mesh, in_specs=in_specs, out_specs=out_specs, check_vma=False)
```

```python
import functools

import jax
import jax.numpy as jnp
from jax import lax
from jax.experimental import pallas as pl
from jax.experimental.pallas import tpu as pltpu
from jax.sharding import PartitionSpec as P

HEAD_DIM = 64
KV_HEADS = 8
GROUP_HEADS = 29
SEQ = 768
HEADS = 6
PAIRS = 3
BLK = 256
NBLK = SEQ // BLK
KV_COLS = KV_HEADS * HEAD_DIM
Q_COLS = HEADS * HEAD_DIM
OWN = 24
CHIP = 48
XROWS = 192
SCALE = 0.125
SCALE_LOG2 = 0.125 * 1.4426950408889634
NEG = -1e30
MESH = pl.DeviceIdType.MESH
F32 = jnp.float32
BF16 = jnp.bfloat16


def dot(a, b):
    return lax.dot_general(a, b, (((1,), (0,)), ((), ())), preferred_element_type=F32)


def dot_t(a, b):
    return lax.dot_general(a, b, (((1,), (1,)), ((), ())), preferred_element_type=F32)


def fold(values, op):
    rows, cols = values.shape
    return op(values.reshape(rows // 8, 8, cols), axis=0)


def pack_rows(rows):
    return jnp.concatenate([rows[:, : KV_COLS // 2], rows[:, KV_COLS // 2 :]], axis=0)


def unpack_rows(block):
    return jnp.concatenate([block[0:OWN], block[OWN:CHIP]], axis=1)


KEY, VALUE = 0, 1


def kernel(
    slots, gates, q_hbm, dy_hbm, key_ref, value_ref,
    dq_hbm, dk_ref, dv_ref, gg_ref,
    shards, k_all, sel_t, k_sel, v_sel, k_sel_t, q_ref, dy_ref, dyg_ref, qn_ref, dyn_ref, dq_ref,
    s_ref, p_ref, dp_ref, ds_ref, scale_ref, delta_ref, gate_acc, gate_recv,
    part, part_recv, chip_sum, x_recv, x_sum, z_recv, first_recv, first_sum, first_x_recv,
    load_sem, store_sem, agz_send, agz_recv, agx_send, agx_recv, agc_send, agc_recv,
    c_send, c_recv, x_send, x_recv_sem, z_send, z_recv_sem, g_send, g_recv, fz_send, fz_recv, fx_send, fx_recv, go,
):
    me = lax.axis_index("head")
    x, z, c = me // 8, (me // 2) % 4, me % 2
    dp = lax.axis_index("dp")
    y, zh = dp // 4, dp % 4

    def head_id(xx, zz, cc):
        return {"head": (xx * 4 + zz) * 2 + cc}

    def dp_id(yy, hh):
        return {"dp": yy * 4 + hh}

    sibling = head_id(x, z, 1 - c)
    near = (z + 1 - 2 * (z % 2), 2 - z // 2, 3 - 3 * (z // 2))

    barrier = pltpu.get_barrier_semaphore()

    def greet(target):
        pl.semaphore_signal(barrier, inc=1, device_id=target, device_id_type=MESH)

    for d in (1, 2, 3):
        greet(head_id(x, (z + d) % 4, c))
        greet(head_id((x + d) % 4, z, c))
        greet(dp_id((y + d) % 4, zh))
    greet(sibling)
    for d in (1, 2, 3):
        pl.when((zh + d) % 4 > zh)(lambda d=d: greet(dp_id(y, (zh + d) % 4)))

    loads = []
    for p in range(PAIRS):
        cols = pl.ds(p * 128, 128)
        loads.append(pltpu.make_async_copy(q_hbm.at[0, :, cols], q_ref.at[p], load_sem.at[0, p]))
        loads.append(pltpu.make_async_copy(dy_hbm.at[0, :, cols], dy_ref.at[p], load_sem.at[1, p]))
    for load in loads:
        load.start()

    shards[KEY, x, c, z] = pack_rows(key_ref[0].astype(F32)).astype(BF16)
    shards[VALUE, x, c, z] = pack_rows(value_ref[0].astype(F32)).astype(BF16)

    pl.semaphore_wait(barrier, 10 + zh)

    sends = []

    def send(copy):
        copy.start()
        sends.append(copy)

    def z_shard(t, source, slot, target):
        return pltpu.make_async_remote_copy(
            src_ref=shards.at[t, x, c, source], dst_ref=shards.at[t, x, c, source],
            send_sem=agz_send.at[t, slot], recv_sem=agz_recv.at[t, source],
            device_id=target, device_id_type=MESH,
        )

    def x_shard(t, xx, zz, slot, d, target):
        return pltpu.make_async_remote_copy(
            src_ref=shards.at[t, xx, c, zz], dst_ref=shards.at[t, xx, c, zz],
            send_sem=agx_send.at[t, slot, d - 1], recv_sem=agx_recv.at[t, xx, zz],
            device_id=target, device_id_type=MESH,
        )

    def c_block(t, xx, cc):
        return pltpu.make_async_remote_copy(
            src_ref=shards.at[t, xx, cc], dst_ref=shards.at[t, xx, cc],
            send_sem=agc_send.at[t, xx], recv_sem=agc_recv.at[t, xx],
            device_id=sibling, device_id_type=MESH,
        )

    def send_z(t):
        for slot, zz in enumerate(near):
            send(z_shard(t, z, slot, head_id(x, zz, c)))

    def send_x(t, slot, zz):
        for d in (1, 3, 2):
            send(x_shard(t, x, zz, slot, d, head_id((x + d) % 4, z, c)))

    def forward_z(t):
        for slot, zz in enumerate(near):
            z_shard(t, zz, slot, sibling).wait_recv()
            send_x(t, slot + 1, zz)
        send(c_block(t, x, c))

    def forward_x(t):
        for d in (1, 3, 2):
            xx = (x + d) % 4
            for zz in (z,) + near:
                x_shard(t, xx, zz, 0, d, sibling).wait_recv()
            send(c_block(t, xx, c))

    send_z(KEY)
    send_x(KEY, 0, z)

    row = lax.broadcasted_iota(jnp.int32, (Q_COLS, KV_COLS), 0)
    col = lax.broadcasted_iota(jnp.int32, (Q_COLS, KV_COLS), 1)
    slot_of_row = row // HEAD_DIM
    group_of_row = jnp.zeros((Q_COLS, KV_COLS), jnp.int32)
    for h in range(HEADS):
        group_of_row = jnp.where(slot_of_row == h, slots[h] // GROUP_HEADS, group_of_row)
    wanted = group_of_row * HEAD_DIM + row % HEAD_DIM
    sel_t[...] = jnp.where(col == wanted, 1.0, 0.0).astype(BF16)

    forward_z(KEY)
    send_z(VALUE)

    for load in loads:
        load.wait()
    low_half = lax.broadcasted_iota(jnp.int32, (1, 128), 1) < HEAD_DIM
    half_masks = (low_half, jnp.logical_not(low_half))
    for p in range(PAIRS):
        gate = jnp.where(low_half, gates[2 * p], gates[2 * p + 1])
        dyg_ref[p] = (dy_ref[p].astype(F32) * gate).astype(BF16)

    def select_x(t, xx):
        c_block(t, xx, 1 - c).wait_recv()
        blocks = []
        for zz in range(4):
            for cc in range(2):
                blocks.append(unpack_rows(shards[t, xx, cc, zz].astype(F32)))
        table = jnp.concatenate(blocks, axis=0).astype(BF16)
        rows = pl.ds(pl.multiple_of(XROWS * xx, XROWS), XROWS)
        if t == KEY:
            k_all[rows, :] = table
        chosen = dot_t(table, sel_t[...]).astype(BF16)
        target = k_sel if t == KEY else v_sel
        for p in range(PAIRS):
            target[p, rows, :] = chosen[:, p * 128 : (p + 1) * 128]

    forward_x(KEY)
    send_x(VALUE, 0, z)
    forward_z(VALUE)
    for d in (1, 2, 3):
        pl.when((zh + d) % 4 < zh)(
            lambda d=d: pl.semaphore_signal(
                go.at[3 - d], inc=1, device_id=dp_id(y, (zh + d) % 4), device_id_type=MESH
            )
        )

    for d in (0, 1, 3, 2):
        select_x(KEY, (x + d) % 4)

    key_pos = lax.broadcasted_iota(jnp.int32, (BLK, BLK), 0)
    query_pos = lax.broadcasted_iota(jnp.int32, (BLK, BLK), 1)
    causal = key_pos <= query_pos
    STEP = 64

    def score_max(i, p, half):
        queries = pl.ds(BLK * i, BLK)
        q_half = jnp.where(half_masks[half], q_ref[p, queries, :], jnp.zeros((), BF16))
        top = jnp.full((8, BLK), NEG, F32)
        for j in range(i + 1):
            keys = pl.ds(BLK * j, BLK)
            s = dot_t(k_sel[p, keys, :], q_half)
            if j == i:
                s = jnp.where(causal, s, NEG)
            top = jnp.maximum(top, fold(s, jnp.max))
            s_ref[half, keys, :] = s
        return jnp.max(top, axis=0, keepdims=True) * SCALE_LOG2

    def exp_block(i, p, half, top):
        queries = pl.ds(BLK * i, BLK)
        h = 2 * p + half
        total = jnp.zeros((8, BLK), F32)
        for k0 in range(0, BLK * (i + 1), STEP):
            keys = pl.ds(k0, STEP)
            e = jnp.exp2(s_ref[half, keys, :] * SCALE_LOG2 - top)
            total = total + fold(e, jnp.sum)
            p_ref[h, keys, queries] = e.astype(BF16)
        inverse = 1.0 / jnp.sum(total, axis=0, keepdims=True)
        scale_ref[h, :, queries] = jnp.broadcast_to(inverse, (8, BLK))
        return jnp.broadcast_to(inverse, (HEAD_DIM, BLK))

    def score_block(i):
        queries = pl.ds(BLK * i, BLK)
        for p in range(PAIRS):
            tops = [score_max(i, p, half) for half in range(2)]
            scales = [exp_block(i, p, half, tops[half]) for half in range(2)]
            scale = jnp.concatenate(scales, axis=0).T
            dyn_ref[p, queries, :] = (dyg_ref[p, queries, :].astype(F32) * scale).astype(BF16)
            qn_ref[p, queries, :] = (q_ref[p, queries, :].astype(F32) * (scale * SCALE)).astype(BF16)

    def weight_grad(i, p, half):
        queries = pl.ds(BLK * i, BLK)
        h = 2 * p + half
        dy_half = jnp.where(half_masks[half], dyg_ref[p, queries, :], jnp.zeros((), BF16))
        weighted = jnp.zeros((8, BLK), F32)
        for j in range(i + 1):
            keys = pl.ds(BLK * j, BLK)
            dp = dot_t(v_sel[p, keys, :], dy_half)
            dp_ref[h, keys, queries] = dp
            weighted = weighted + fold(p_ref[h, keys, queries].astype(F32) * dp, jnp.sum)
        delta = jnp.sum(weighted, axis=0, keepdims=True) * scale_ref[h, 0:1, queries]
        delta_ref[h, :, queries] = jnp.broadcast_to(delta, (8, BLK))
        gate_acc[0, h : h + 1, :] = (
            gate_acc[0, h : h + 1, :] + delta[:, 0:128] + delta[:, 128:256]
        )

    def score_grad(i, p, half):
        queries = pl.ds(BLK * i, BLK)
        h = 2 * p + half
        depth = BLK * (i + 1)
        delta = delta_ref[h, 0:1, queries]
        for k0 in range(0, depth, STEP):
            keys = pl.ds(k0, STEP)
            ds_ref[h, keys, queries] = (
                p_ref[h, keys, queries].astype(F32) * (dp_ref[h, keys, queries] - delta)
            ).astype(BF16)

    def query_grad_t(i, p, half):
        queries = pl.ds(BLK * i, BLK)
        h = 2 * p + half
        depth = BLK * (i + 1)
        return (SCALE * scale_ref[h, 0:1, queries]) * dot(
            k_sel_t[p, half * 64 : (half + 1) * 64, 0:depth], ds_ref[h, 0:depth, queries]
        )

    def grad_block(i):
        queries = pl.ds(BLK * i, BLK)
        for p in range(PAIRS):
            for half in range(2):
                score_grad(i, p, half)
            dq_t = [query_grad_t(i, p, half) for half in range(2)]
            dq_ref[p, queries, :] = jnp.concatenate(dq_t, axis=0).T.astype(BF16)

    stores = []

    def store_queries(i):
        for p in range(PAIRS):
            copy = pltpu.make_async_copy(
                dq_ref.at[p, pl.ds(BLK * i, BLK), :],
                dq_hbm.at[0, pl.ds(BLK * i, BLK), pl.ds(128 * p, 128)],
                store_sem.at[i, p],
            )
            copy.start()
            stores.append(copy)

    def split(lo, hi):
        cuts = sorted({lo, hi} | {b for b in range(0, SEQ, BLK) if lo < b < hi})
        return list(zip(cuts[:-1], cuts[1:]))

    def head_grads(weights_ref, other_ref, lo, hi):
        pieces = []
        for a, b in split(lo, hi):
            start = (a // BLK) * BLK
            row_parts = []
            for p in range(PAIRS):
                even = dot(weights_ref[2 * p, a:b, start:SEQ], other_ref[p, start:SEQ, :])
                odd = dot(weights_ref[2 * p + 1, a:b, start:SEQ], other_ref[p, start:SEQ, :])
                row_parts.append(jnp.where(low_half, even, odd))
            pieces.append(jnp.concatenate(row_parts, axis=1))
        return jnp.concatenate(pieces, axis=0)

    def chip_copy(t, xx):
        return pltpu.make_async_remote_copy(
            src_ref=part.at[t, xx, 1 - c], dst_ref=part_recv.at[t, xx],
            send_sem=c_send.at[t, xx], recv_sem=c_recv.at[t, xx],
            device_id=sibling, device_id_type=MESH,
        )

    def x_copy(t, xx):
        return pltpu.make_async_remote_copy(
            src_ref=chip_sum.at[t, xx], dst_ref=x_recv.at[t, x],
            send_sem=x_send.at[t, xx], recv_sem=x_recv_sem.at[t, x],
            device_id=head_id(xx, z, c), device_id_type=MESH,
        )

    def z_copy(t, slot, zz):
        return pltpu.make_async_remote_copy(
            src_ref=x_sum.at[t, zz], dst_ref=z_recv.at[t, z],
            send_sem=z_send.at[t, slot], recv_sem=z_recv_sem.at[t, z],
            device_id=head_id(x, zz, c), device_id_type=MESH,
        )

    def key_block(t, xx):
        lo, hi = XROWS * xx, XROWS * (xx + 1)
        if t == KEY:
            grads = head_grads(ds_ref, qn_ref, lo, hi)
        else:
            grads = head_grads(p_ref, dyn_ref, lo, hi)
        grads = dot(grads.astype(BF16), sel_t[...])
        for zz in range(4):
            for cc in range(2):
                at = CHIP * zz + OWN * cc
                part[t, xx, cc, zz] = pack_rows(grads[at : at + OWN]).astype(BF16)
        send(chip_copy(t, xx))

    def chip_add(t, xx):
        chip_copy(t, xx).wait_recv()
        for zz in range(4):
            chip_sum[t, xx, zz] = (
                part[t, xx, c, zz].astype(F32) + part_recv[t, xx, zz].astype(F32)
            ).astype(BF16)

        if (t, xx) != (KEY, 0):

            @pl.when(xx != x)
            def _():
                x_copy(t, xx).start()

    def x_add(t):
        for d in (1, 3, 2):
            src = (x + d) % 4
            pltpu.make_async_remote_copy(
                src_ref=chip_sum.at[t, src], dst_ref=x_recv.at[t, src],
                send_sem=x_send.at[t, src], recv_sem=x_recv_sem.at[t, src],
                device_id=head_id(src, z, c), device_id_type=MESH,
            ).wait_recv()
        for slot, zz in enumerate(near + (z,)):
            total = chip_sum[t, x, zz].astype(F32)
            for dx in (1, 2, 3):
                total = total + x_recv[t, (x + dx) % 4, zz].astype(F32)
            x_sum[t, zz] = total.astype(BF16)
            if slot < 3 and t == KEY:
                z_copy(t, slot, zz).start()
            elif slot < 3:
                send(z_copy(t, slot, zz))

    def z_add(t, out_ref):
        total = x_sum[t, z].astype(F32)
        for slot, zz in enumerate(near):
            pltpu.make_async_remote_copy(
                src_ref=x_sum.at[t, zz], dst_ref=z_recv.at[t, zz],
                send_sem=z_send.at[t, slot], recv_sem=z_recv_sem.at[t, zz],
                device_id=head_id(x, zz, c), device_id_type=MESH,
            ).wait_recv()
            total = total + z_recv[t, zz].astype(F32)
        out_ref[0] = unpack_rows(total).astype(BF16)

    def first_z_copy(slot, zz):
        return pltpu.make_async_remote_copy(
            src_ref=chip_sum.at[KEY, 0, zz], dst_ref=first_recv.at[z],
            send_sem=fz_send.at[slot], recv_sem=fz_recv.at[z],
            device_id=head_id(x, zz, c), device_id_type=MESH,
        )

    def first_z_wait(slot, zz):
        pltpu.make_async_remote_copy(
            src_ref=chip_sum.at[KEY, 0, zz], dst_ref=first_recv.at[zz],
            send_sem=fz_send.at[slot], recv_sem=fz_recv.at[zz],
            device_id=head_id(x, zz, c), device_id_type=MESH,
        ).wait_recv()

    def first_x_copy(xx):
        return pltpu.make_async_remote_copy(
            src_ref=first_sum, dst_ref=first_x_recv.at[xx],
            send_sem=fx_send.at[0], recv_sem=fx_recv.at[xx],
            device_id=head_id(0, z, c), device_id_type=MESH,
        )

    def gate_copy(stage, d, target):
        return pltpu.make_async_remote_copy(
            src_ref=gate_acc.at[stage], dst_ref=gate_recv.at[stage, d - 1],
            send_sem=g_send.at[stage, d - 1], recv_sem=g_recv.at[stage, d - 1],
            device_id=target, device_id_type=MESH,
        )

    def gate_add(stage):
        total = gate_acc[stage]
        for d in (1, 2, 3):
            gate_copy(stage, d, sibling).wait_recv()
            total = total + gate_recv[stage, d - 1]
        return total

    gate_acc[0] = jnp.zeros((8, 128), F32)

    score_block(2)
    key_block(VALUE, 3)
    score_block(1)
    chip_add(VALUE, 3)
    key_block(VALUE, 2)
    forward_x(VALUE)
    score_block(0)
    chip_add(VALUE, 2)

    k_sel_t_all = dot_t(sel_t[...], k_all[...]).astype(BF16)
    for p in range(PAIRS):
        k_sel_t[p] = k_sel_t_all[p * 128 : (p + 1) * 128, :]
    for d in (0, 1, 3, 2):
        select_x(VALUE, (x + d) % 4)
    for i in (2, 1, 0):
        for p in range(PAIRS):
            for half in range(2):
                weight_grad(i, p, half)

    for d in (1, 2, 3):
        send(gate_copy(0, d, dp_id((y + d) % 4, zh)))
    key_block(VALUE, 1)
    key_block(VALUE, 0)
    chip_add(VALUE, 1)
    gate_acc[1] = gate_add(0)
    for d in (1, 2, 3):
        pl.when((zh + d) % 4 > zh)(lambda d=d: pl.semaphore_wait(go.at[d - 1], 1))
    for d in (1, 2, 3):
        send(gate_copy(1, d, dp_id(y, (zh + d) % 4)))

    grad_block(2)
    chip_add(VALUE, 0)
    key_block(KEY, 3)
    store_queries(2)
    grad_block(1)
    chip_add(KEY, 3)
    key_block(KEY, 2)
    store_queries(1)
    grad_block(0)
    chip_add(KEY, 2)
    key_block(KEY, 1)
    store_queries(0)
    key_block(KEY, 0)
    chip_add(KEY, 1)
    chip_add(KEY, 0)
    for slot, zz in enumerate(near):
        send(first_z_copy(slot, zz))
    x_add(VALUE)
    first = chip_sum[KEY, 0, z].astype(F32)
    for slot, zz in enumerate(near):
        first_z_wait(slot, zz)
        first = first + first_recv[zz].astype(F32)
    first_sum[...] = first.astype(BF16)

    @pl.when(x != 0)
    def _():
        first_x_copy(x).start()
        x_add(KEY)
        z_add(KEY, dk_ref)
        for slot, zz in enumerate(near):
            z_copy(KEY, slot, zz).wait_send()
        first_x_copy(x).wait_send()

    @pl.when(x == 0)
    def _():
        total = first_sum[...].astype(F32)
        for xx in (3, 1, 2):
            first_x_copy(xx).wait_recv()
            total = total + first_x_recv[xx].astype(F32)
        dk_ref[0] = unpack_rows(total).astype(BF16)

    z_add(VALUE, dv_ref)
    gate_sum = gate_add(1)
    for h in range(HEADS):
        gg_ref[h] = jnp.sum(gate_sum[h : h + 1, :]) / (16.0 * gates[h])

    for xx in range(4):
        for t in (KEY, VALUE):
            if (t, xx) != (KEY, 0):
                pl.when(xx != x)(lambda t=t, xx=xx: x_copy(t, xx).wait_send())
    for copy in sends:
        copy.wait_send()
    for copy in stores:
        copy.wait()


def finish(*refs):
    ins, outs, held = refs[:4], refs[4:8], refs[8:12]
    sem_in, sem_out = refs[12:]
    parts = [(n, pl.ds(BLK * k, BLK)) for k, n in enumerate((0, 0, 0))] + [(1, None), (2, None), (3, None)]

    def view(ref, rows):
        return ref if rows is None else ref.at[0, rows, :]

    fetch, store = [], []
    for k, (n, rows) in enumerate(parts):
        here = view(held[n], rows)
        fetch.append(pltpu.make_async_copy(view(ins[n], rows), here, sem_in.at[k]))
        store.append(pltpu.make_async_copy(here, view(outs[n], rows), sem_out.at[k]))
    for copy in fetch:
        copy.start()
    for first, second in zip(fetch, store):
        first.wait()
        second.start()
    for copy in store:
        copy.wait()


def local(queries, key_rows, value_rows, upstream, head_gate, slot_heads):
    vmem = pl.BlockSpec(memory_space=pltpu.VMEM)
    smem = pl.BlockSpec(memory_space=pltpu.SMEM)
    hbm = pl.BlockSpec(memory_space=pl.ANY)
    dma = pltpu.SemaphoreType.DMA
    out_shape = (
        jax.ShapeDtypeStruct(queries.shape, BF16),
        jax.ShapeDtypeStruct(key_rows.shape, BF16),
        jax.ShapeDtypeStruct(value_rows.shape, BF16),
        jax.ShapeDtypeStruct(head_gate.shape, F32),
    )
    half = KV_COLS // 2
    rows_of_pair = pltpu.VMEM((PAIRS, SEQ, 128), BF16)
    results = pl.pallas_call(
        kernel,
        out_shape=out_shape,
        in_specs=[smem, smem, hbm, hbm, vmem, vmem],
        out_specs=(hbm, vmem, vmem, smem),
        scratch_shapes=[
            pltpu.VMEM((2, 4, 2, 4, CHIP, half), BF16),
            pltpu.VMEM((SEQ, KV_COLS), BF16),
            pltpu.VMEM((Q_COLS, KV_COLS), BF16),
            rows_of_pair, rows_of_pair,
            pltpu.VMEM((PAIRS, 128, SEQ), BF16),
            rows_of_pair, rows_of_pair, rows_of_pair, rows_of_pair, rows_of_pair, rows_of_pair,
            pltpu.VMEM((2, SEQ, BLK), F32),
            pltpu.VMEM((HEADS, SEQ, SEQ), BF16),
            pltpu.VMEM((HEADS, SEQ, SEQ), F32),
            pltpu.VMEM((HEADS, SEQ, SEQ), BF16),
            pltpu.VMEM((HEADS, 8, SEQ), F32),
            pltpu.VMEM((HEADS, 8, SEQ), F32),
            pltpu.VMEM((2, 8, 128), F32),
            pltpu.VMEM((2, 3, 8, 128), F32),
            pltpu.VMEM((2, 4, 2, 4, CHIP, half), BF16),
            pltpu.VMEM((2, 4, 4, CHIP, half), BF16),
            pltpu.VMEM((2, 4, 4, CHIP, half), BF16),
            pltpu.VMEM((2, 4, 4, CHIP, half), BF16),
            pltpu.VMEM((2, 4, CHIP, half), BF16),
            pltpu.VMEM((2, 4, CHIP, half), BF16),
            pltpu.VMEM((4, CHIP, half), BF16),
            pltpu.VMEM((CHIP, half), BF16),
            pltpu.VMEM((4, CHIP, half), BF16),
            dma((2, PAIRS)), dma((NBLK, PAIRS)),
            dma((2, 3)), dma((2, 4)), dma((2, 4, 3)), dma((2, 4, 4)), dma((2, 4)), dma((2, 4)),
            dma((2, 4)), dma((2, 4)), dma((2, 4)), dma((2, 4)), dma((2, 3)), dma((2, 4)),
            dma((2, 3)), dma((2, 3)), dma((3,)), dma((4,)), dma((1,)), dma((4,)),
            pltpu.SemaphoreType.REGULAR((3,)),
        ],
        compiler_params=pltpu.CompilerParams(
            collective_id=0, has_side_effects=True, vmem_limit_bytes=58 * 1024 * 1024
        ),
        name="attention_backward",
    )(slot_heads, head_gate, queries, upstream, key_rows, value_rows)
    return pl.pallas_call(
        finish,
        out_shape=out_shape,
        in_specs=[hbm] * 4,
        out_specs=(hbm,) * 4,
        scratch_shapes=[
            pltpu.VMEM(queries.shape, BF16),
            pltpu.VMEM(key_rows.shape, BF16),
            pltpu.VMEM(value_rows.shape, BF16),
            pltpu.SMEM(head_gate.shape, F32),
            dma((6,)), dma((6,)),
        ],
        name="copy_out",
    )(*results)


def solution(mesh):
    in_specs = (
        P("dp", None, "head"),
        P("dp", "head", None),
        P("dp", "head", None),
        P("dp", None, "head"),
        P("head"),
        P("head"),
    )
    out_specs = (P("dp", None, "head"), P("dp", "head", None), P("dp", "head", None), P("head"))
    return jax.shard_map(local, mesh=mesh, in_specs=in_specs, out_specs=out_specs, check_vma=False)
```

```python
import functools

import jax
import jax.numpy as jnp
from jax import lax
from jax.experimental import pallas as pl
from jax.experimental.pallas import tpu as pltpu
from jax.sharding import PartitionSpec as P

HEAD_DIM = 64
KV_HEADS = 8
GROUP_HEADS = 29
SEQ = 768
HEADS = 6
PAIRS = 3
BLK = 256
NBLK = SEQ // BLK
KV_COLS = KV_HEADS * HEAD_DIM
Q_COLS = HEADS * HEAD_DIM
OWN = 24
CHIP = 48
XROWS = 192
SCALE = 0.125
SCALE_LOG2 = 0.125 * 1.4426950408889634
NEG = -1e30
MESH = pl.DeviceIdType.MESH
F32 = jnp.float32
BF16 = jnp.bfloat16


def dot(a, b):
    return lax.dot_general(a, b, (((1,), (0,)), ((), ())), preferred_element_type=F32)


def dot_t(a, b):
    return lax.dot_general(a, b, (((1,), (1,)), ((), ())), preferred_element_type=F32)


def fold(values, op):
    rows, cols = values.shape
    return op(values.reshape(rows // 8, 8, cols), axis=0)


def pack_rows(rows):
    return jnp.concatenate([rows[:, : KV_COLS // 2], rows[:, KV_COLS // 2 :]], axis=0)


def unpack_rows(block):
    return jnp.concatenate([block[0:OWN], block[OWN:CHIP]], axis=1)


KEY, VALUE = 0, 1


def kernel(
    slots_hbm, gates_hbm, q_hbm, dy_hbm, key_hbm, value_hbm,
    dq_hbm, dk_hbm, dv_hbm, gg_hbm,
    slots, gates, key_ref, value_ref, dk_ref, dv_ref, gg_ref, small_in, small_out,
    shards, k_all, sel_t, k_sel, v_sel, k_sel_t, q_ref, dy_ref, dyg_ref, qn_ref, dyn_ref, dq_ref,
    p_ref, dp_ref, ds_ref, scale_ref, delta_ref, gate_acc, gate_recv,
    part, part_recv, chip_sum, x_recv, x_sum, z_recv, first_recv, first_sum, first_x_recv,
    load_sem, store_sem, agz_send, agz_recv, agx_send, agx_recv, agc_send, agc_recv,
    c_send, c_recv, x_send, x_recv_sem, z_send, z_recv_sem, g_send, g_recv, fz_send, fz_recv, fx_send, fx_recv, go,
):
    me = lax.axis_index("head")
    x, z, c = me // 8, (me // 2) % 4, me % 2
    dp = lax.axis_index("dp")
    y, zh = dp // 4, dp % 4

    def head_id(xx, zz, cc):
        return {"head": (xx * 4 + zz) * 2 + cc}

    def dp_id(yy, hh):
        return {"dp": yy * 4 + hh}

    sibling = head_id(x, z, 1 - c)
    near = (z + 1 - 2 * (z % 2), 2 - z // 2, 3 - 3 * (z // 2))

    fetches = [
        pltpu.make_async_copy(there, here, small_in.at[n])
        for n, (there, here) in enumerate(
            ((key_hbm, key_ref), (value_hbm, value_ref), (slots_hbm, slots), (gates_hbm, gates))
        )
    ]
    for fetch in fetches:
        fetch.start()

    barrier = pltpu.get_barrier_semaphore()

    def greet(target):
        pl.semaphore_signal(barrier, inc=1, device_id=target, device_id_type=MESH)

    for d in (1, 2, 3):
        greet(head_id(x, (z + d) % 4, c))
        greet(head_id((x + d) % 4, z, c))
        greet(dp_id((y + d) % 4, zh))
    greet(sibling)
    for d in (1, 2, 3):
        pl.when((zh + d) % 4 > zh)(lambda d=d: greet(dp_id(y, (zh + d) % 4)))

    loads = []
    for p in range(PAIRS):
        cols = pl.ds(p * 128, 128)
        loads.append(pltpu.make_async_copy(q_hbm.at[0, :, cols], q_ref.at[p], load_sem.at[0, p]))
        loads.append(pltpu.make_async_copy(dy_hbm.at[0, :, cols], dy_ref.at[p], load_sem.at[1, p]))
    for load in loads:
        load.start()

    for fetch in fetches:
        fetch.wait()
    shards[KEY, x, c, z] = pack_rows(key_ref[0].astype(F32)).astype(BF16)
    shards[VALUE, x, c, z] = pack_rows(value_ref[0].astype(F32)).astype(BF16)

    pl.semaphore_wait(barrier, 10 + zh)

    sends = []

    def send(copy):
        copy.start()
        sends.append(copy)

    def z_shard(t, source, slot, target):
        return pltpu.make_async_remote_copy(
            src_ref=shards.at[t, x, c, source], dst_ref=shards.at[t, x, c, source],
            send_sem=agz_send.at[t, slot], recv_sem=agz_recv.at[t, source],
            device_id=target, device_id_type=MESH,
        )

    def x_shard(t, xx, zz, slot, d, target):
        return pltpu.make_async_remote_copy(
            src_ref=shards.at[t, xx, c, zz], dst_ref=shards.at[t, xx, c, zz],
            send_sem=agx_send.at[t, slot, d - 1], recv_sem=agx_recv.at[t, xx, zz],
            device_id=target, device_id_type=MESH,
        )

    def c_block(t, xx, cc):
        return pltpu.make_async_remote_copy(
            src_ref=shards.at[t, xx, cc], dst_ref=shards.at[t, xx, cc],
            send_sem=agc_send.at[t, xx], recv_sem=agc_recv.at[t, xx],
            device_id=sibling, device_id_type=MESH,
        )

    def send_z(t):
        for slot, zz in enumerate(near):
            send(z_shard(t, z, slot, head_id(x, zz, c)))

    def send_x(t, slot, zz):
        for d in (1, 3, 2):
            send(x_shard(t, x, zz, slot, d, head_id((x + d) % 4, z, c)))

    def forward_z(t):
        for slot, zz in enumerate(near):
            z_shard(t, zz, slot, sibling).wait_recv()
            send_x(t, slot + 1, zz)
        send(c_block(t, x, c))

    def forward_x(t):
        for d in (1, 3, 2):
            xx = (x + d) % 4
            for zz in (z,) + near:
                x_shard(t, xx, zz, 0, d, sibling).wait_recv()
            send(c_block(t, xx, c))

    send_z(KEY)
    send_x(KEY, 0, z)

    row = lax.broadcasted_iota(jnp.int32, (Q_COLS, KV_COLS), 0)
    col = lax.broadcasted_iota(jnp.int32, (Q_COLS, KV_COLS), 1)
    slot_of_row = row // HEAD_DIM
    group_of_row = jnp.zeros((Q_COLS, KV_COLS), jnp.int32)
    for h in range(HEADS):
        group_of_row = jnp.where(slot_of_row == h, slots[h] // GROUP_HEADS, group_of_row)
    wanted = group_of_row * HEAD_DIM + row % HEAD_DIM
    sel_t[...] = jnp.where(col == wanted, 1.0, 0.0).astype(BF16)

    forward_z(KEY)
    send_z(VALUE)

    for load in loads:
        load.wait()
    low_half = lax.broadcasted_iota(jnp.int32, (1, 128), 1) < HEAD_DIM
    half_masks = (low_half, jnp.logical_not(low_half))
    for p in range(PAIRS):
        gate = jnp.where(low_half, gates[2 * p], gates[2 * p + 1])
        dyg_ref[p] = (dy_ref[p].astype(F32) * gate).astype(BF16)

    def select_x(t, xx):
        c_block(t, xx, 1 - c).wait_recv()
        blocks = []
        for zz in range(4):
            for cc in range(2):
                blocks.append(unpack_rows(shards[t, xx, cc, zz].astype(F32)))
        table = jnp.concatenate(blocks, axis=0).astype(BF16)
        rows = pl.ds(pl.multiple_of(XROWS * xx, XROWS), XROWS)
        if t == KEY:
            k_all[rows, :] = table
        chosen = dot_t(table, sel_t[...]).astype(BF16)
        target = k_sel if t == KEY else v_sel
        for p in range(PAIRS):
            target[p, rows, :] = chosen[:, p * 128 : (p + 1) * 128]

    forward_x(KEY)
    send_x(VALUE, 0, z)
    forward_z(VALUE)
    for d in (1, 2, 3):
        pl.when((zh + d) % 4 < zh)(
            lambda d=d: pl.semaphore_signal(
                go.at[3 - d], inc=1, device_id=dp_id(y, (zh + d) % 4), device_id_type=MESH
            )
        )

    for d in (0, 1, 3, 2):
        select_x(KEY, (x + d) % 4)

    key_pos = lax.broadcasted_iota(jnp.int32, (BLK, BLK), 0)
    query_pos = lax.broadcasted_iota(jnp.int32, (BLK, BLK), 1)
    causal = key_pos <= query_pos
    STEP = 64

    def score_max(i, p, half):
        queries = pl.ds(BLK * i, BLK)
        q_half = jnp.where(half_masks[half], q_ref[p, queries, :], jnp.zeros((), BF16))
        top = jnp.full((8, BLK), NEG, F32)
        for j in range(i + 1):
            keys = pl.ds(BLK * j, BLK)
            s = dot_t(k_sel[p, keys, :], q_half)
            if j == i:
                s = jnp.where(causal, s, NEG)
            top = jnp.maximum(top, fold(s, jnp.max))
            dp_ref[2 * p + half, keys, queries] = s
        return jnp.max(top, axis=0, keepdims=True) * SCALE_LOG2

    def exp_block(i, p, half, top):
        queries = pl.ds(BLK * i, BLK)
        h = 2 * p + half
        total = jnp.zeros((8, BLK), F32)
        for k0 in range(0, BLK * (i + 1), STEP):
            keys = pl.ds(k0, STEP)
            e = jnp.exp2(dp_ref[h, keys, queries] * SCALE_LOG2 - top)
            total = total + fold(e, jnp.sum)
            p_ref[h, keys, queries] = e.astype(BF16)
        inverse = 1.0 / jnp.sum(total, axis=0, keepdims=True)
        scale_ref[h, :, queries] = jnp.broadcast_to(inverse, (8, BLK))
        return jnp.broadcast_to(inverse, (HEAD_DIM, BLK))

    def score_block(i):
        queries = pl.ds(BLK * i, BLK)
        for p in range(PAIRS):
            tops = [score_max(i, p, half) for half in range(2)]
            scales = [exp_block(i, p, half, tops[half]) for half in range(2)]
            scale = jnp.concatenate(scales, axis=0).T
            dyn_ref[p, queries, :] = (dyg_ref[p, queries, :].astype(F32) * scale).astype(BF16)
            qn_ref[p, queries, :] = (q_ref[p, queries, :].astype(F32) * (scale * SCALE)).astype(BF16)

    def weight_grad(i, p, half):
        queries = pl.ds(BLK * i, BLK)
        h = 2 * p + half
        dy_half = jnp.where(half_masks[half], dyg_ref[p, queries, :], jnp.zeros((), BF16))
        weighted = jnp.zeros((8, BLK), F32)
        for j in range(i + 1):
            keys = pl.ds(BLK * j, BLK)
            dp = dot_t(v_sel[p, keys, :], dy_half)
            dp_ref[h, keys, queries] = dp
            weighted = weighted + fold(p_ref[h, keys, queries].astype(F32) * dp, jnp.sum)
        delta = jnp.sum(weighted, axis=0, keepdims=True) * scale_ref[h, 0:1, queries]
        delta_ref[h, :, queries] = jnp.broadcast_to(delta, (8, BLK))
        gate_acc[0, h : h + 1, :] = (
            gate_acc[0, h : h + 1, :] + delta[:, 0:128] + delta[:, 128:256]
        )

    def score_grad(i, p, half):
        queries = pl.ds(BLK * i, BLK)
        h = 2 * p + half
        depth = BLK * (i + 1)
        delta = delta_ref[h, 0:1, queries]
        for k0 in range(0, depth, STEP):
            keys = pl.ds(k0, STEP)
            ds_ref[h, keys, queries] = (
                p_ref[h, keys, queries].astype(F32) * (dp_ref[h, keys, queries] - delta)
            ).astype(BF16)

    def query_grad_t(i, p, half):
        queries = pl.ds(BLK * i, BLK)
        h = 2 * p + half
        depth = BLK * (i + 1)
        return (SCALE * scale_ref[h, 0:1, queries]) * dot(
            k_sel_t[p, half * 64 : (half + 1) * 64, 0:depth], ds_ref[h, 0:depth, queries]
        )

    def grad_block(i):
        queries = pl.ds(BLK * i, BLK)
        for p in range(PAIRS):
            for half in range(2):
                score_grad(i, p, half)
            dq_t = [query_grad_t(i, p, half) for half in range(2)]
            dq_ref[p, queries, :] = jnp.concatenate(dq_t, axis=0).T.astype(BF16)

    stores = []

    def store_queries(i):
        for p in range(PAIRS):
            copy = pltpu.make_async_copy(
                dq_ref.at[p, pl.ds(BLK * i, BLK), :],
                dq_hbm.at[0, pl.ds(BLK * i, BLK), pl.ds(128 * p, 128)],
                store_sem.at[i, p],
            )
            copy.start()
            stores.append(copy)

    def split(lo, hi):
        cuts = sorted({lo, hi} | {b for b in range(0, SEQ, BLK) if lo < b < hi})
        return list(zip(cuts[:-1], cuts[1:]))

    def head_grads(weights_ref, other_ref, lo, hi):
        pieces = []
        for a, b in split(lo, hi):
            start = (a // BLK) * BLK
            row_parts = []
            for p in range(PAIRS):
                even = dot(weights_ref[2 * p, a:b, start:SEQ], other_ref[p, start:SEQ, :])
                odd = dot(weights_ref[2 * p + 1, a:b, start:SEQ], other_ref[p, start:SEQ, :])
                row_parts.append(jnp.where(low_half, even, odd))
            pieces.append(jnp.concatenate(row_parts, axis=1))
        return jnp.concatenate(pieces, axis=0)

    def chip_copy(t, xx):
        return pltpu.make_async_remote_copy(
            src_ref=part.at[t, xx, 1 - c], dst_ref=part_recv.at[t, xx],
            send_sem=c_send.at[t, xx], recv_sem=c_recv.at[t, xx],
            device_id=sibling, device_id_type=MESH,
        )

    def x_copy(t, xx):
        return pltpu.make_async_remote_copy(
            src_ref=chip_sum.at[t, xx], dst_ref=x_recv.at[t, x],
            send_sem=x_send.at[t, xx], recv_sem=x_recv_sem.at[t, x],
            device_id=head_id(xx, z, c), device_id_type=MESH,
        )

    def z_copy(t, slot, zz):
        return pltpu.make_async_remote_copy(
            src_ref=x_sum.at[t, zz], dst_ref=z_recv.at[t, z],
            send_sem=z_send.at[t, slot], recv_sem=z_recv_sem.at[t, z],
            device_id=head_id(x, zz, c), device_id_type=MESH,
        )

    def key_block(t, xx):
        lo, hi = XROWS * xx, XROWS * (xx + 1)
        if t == KEY:
            grads = head_grads(ds_ref, qn_ref, lo, hi)
        else:
            grads = head_grads(p_ref, dyn_ref, lo, hi)
        grads = dot(grads.astype(BF16), sel_t[...])
        for zz in range(4):
            for cc in range(2):
                at = CHIP * zz + OWN * cc
                part[t, xx, cc, zz] = pack_rows(grads[at : at + OWN]).astype(BF16)
        send(chip_copy(t, xx))

    def chip_add(t, xx):
        chip_copy(t, xx).wait_recv()
        for zz in range(4):
            chip_sum[t, xx, zz] = (
                part[t, xx, c, zz].astype(F32) + part_recv[t, xx, zz].astype(F32)
            ).astype(BF16)

        if (t, xx) != (KEY, 0):

            @pl.when(xx != x)
            def _():
                x_copy(t, xx).start()

    def x_add(t):
        for d in (1, 3, 2):
            src = (x + d) % 4
            pltpu.make_async_remote_copy(
                src_ref=chip_sum.at[t, src], dst_ref=x_recv.at[t, src],
                send_sem=x_send.at[t, src], recv_sem=x_recv_sem.at[t, src],
                device_id=head_id(src, z, c), device_id_type=MESH,
            ).wait_recv()
        for slot, zz in enumerate(near + (z,)):
            total = chip_sum[t, x, zz].astype(F32)
            for dx in (1, 2, 3):
                total = total + x_recv[t, (x + dx) % 4, zz].astype(F32)
            x_sum[t, zz] = total.astype(BF16)
            if slot < 3 and t == KEY:
                z_copy(t, slot, zz).start()
            elif slot < 3:
                send(z_copy(t, slot, zz))

    def z_add(t, out_ref):
        total = x_sum[t, z].astype(F32)
        for slot, zz in enumerate(near):
            pltpu.make_async_remote_copy(
                src_ref=x_sum.at[t, zz], dst_ref=z_recv.at[t, zz],
                send_sem=z_send.at[t, slot], recv_sem=z_recv_sem.at[t, zz],
                device_id=head_id(x, zz, c), device_id_type=MESH,
            ).wait_recv()
            total = total + z_recv[t, zz].astype(F32)
        out_ref[0] = unpack_rows(total).astype(BF16)

    def first_z_copy(slot, zz):
        return pltpu.make_async_remote_copy(
            src_ref=chip_sum.at[KEY, 0, zz], dst_ref=first_recv.at[z],
            send_sem=fz_send.at[slot], recv_sem=fz_recv.at[z],
            device_id=head_id(x, zz, c), device_id_type=MESH,
        )

    def first_z_wait(slot, zz):
        pltpu.make_async_remote_copy(
            src_ref=chip_sum.at[KEY, 0, zz], dst_ref=first_recv.at[zz],
            send_sem=fz_send.at[slot], recv_sem=fz_recv.at[zz],
            device_id=head_id(x, zz, c), device_id_type=MESH,
        ).wait_recv()

    def first_x_copy(xx):
        return pltpu.make_async_remote_copy(
            src_ref=first_sum, dst_ref=first_x_recv.at[xx],
            send_sem=fx_send.at[0], recv_sem=fx_recv.at[xx],
            device_id=head_id(0, z, c), device_id_type=MESH,
        )

    def gate_copy(stage, d, target):
        return pltpu.make_async_remote_copy(
            src_ref=gate_acc.at[stage], dst_ref=gate_recv.at[stage, d - 1],
            send_sem=g_send.at[stage, d - 1], recv_sem=g_recv.at[stage, d - 1],
            device_id=target, device_id_type=MESH,
        )

    def gate_add(stage):
        total = gate_acc[stage]
        for d in (1, 2, 3):
            gate_copy(stage, d, sibling).wait_recv()
            total = total + gate_recv[stage, d - 1]
        return total

    gate_acc[0] = jnp.zeros((8, 128), F32)

    score_block(2)
    key_block(VALUE, 3)
    score_block(1)
    chip_add(VALUE, 3)
    key_block(VALUE, 2)
    score_block(0)
    forward_x(VALUE)
    chip_add(VALUE, 2)

    k_sel_t_all = dot_t(sel_t[...], k_all[...]).astype(BF16)
    for p in range(PAIRS):
        k_sel_t[p] = k_sel_t_all[p * 128 : (p + 1) * 128, :]
    for d in (0, 1, 3, 2):
        select_x(VALUE, (x + d) % 4)
    for i in (2, 1, 0):
        for p in range(PAIRS):
            for half in range(2):
                weight_grad(i, p, half)

    for d in (1, 2, 3):
        send(gate_copy(0, d, dp_id((y + d) % 4, zh)))
    key_block(VALUE, 1)
    key_block(VALUE, 0)
    chip_add(VALUE, 1)
    gate_acc[1] = gate_add(0)
    for d in (1, 2, 3):
        pl.when((zh + d) % 4 > zh)(lambda d=d: pl.semaphore_wait(go.at[d - 1], 1))
    for d in (1, 2, 3):
        send(gate_copy(1, d, dp_id(y, (zh + d) % 4)))

    grad_block(2)
    chip_add(VALUE, 0)
    key_block(KEY, 3)
    store_queries(2)
    grad_block(1)
    chip_add(KEY, 3)
    key_block(KEY, 2)
    store_queries(1)
    grad_block(0)
    chip_add(KEY, 2)
    key_block(KEY, 1)
    store_queries(0)
    key_block(KEY, 0)
    chip_add(KEY, 1)
    chip_add(KEY, 0)
    for slot, zz in enumerate(near):
        send(first_z_copy(slot, zz))
    x_add(VALUE)
    first = chip_sum[KEY, 0, z].astype(F32)
    for slot, zz in enumerate(near):
        first_z_wait(slot, zz)
        first = first + first_recv[zz].astype(F32)
    first_sum[...] = first.astype(BF16)

    def store_small(n, here, there):
        copy = pltpu.make_async_copy(here, there, small_out.at[n])
        copy.start()
        stores.append(copy)

    @pl.when(x != 0)
    def _():
        first_x_copy(x).start()
        x_add(KEY)

    z_add(VALUE, dv_ref)
    store_small(0, dv_ref, dv_hbm)
    gate_sum = gate_add(1)
    for h in range(HEADS):
        gg_ref[h] = jnp.sum(gate_sum[h : h + 1, :]) / (16.0 * gates[h])
    store_small(1, gg_ref, gg_hbm)

    @pl.when(x != 0)
    def _():
        z_add(KEY, dk_ref)
        for slot, zz in enumerate(near):
            z_copy(KEY, slot, zz).wait_send()
        first_x_copy(x).wait_send()

    @pl.when(x == 0)
    def _():
        total = first_sum[...].astype(F32)
        for xx in (3, 1, 2):
            first_x_copy(xx).wait_recv()
            total = total + first_x_recv[xx].astype(F32)
        dk_ref[0] = unpack_rows(total).astype(BF16)

    store_small(2, dk_ref, dk_hbm)
    for xx in range(4):
        for t in (KEY, VALUE):
            if (t, xx) != (KEY, 0):
                pl.when(xx != x)(lambda t=t, xx=xx: x_copy(t, xx).wait_send())
    for copy in sends:
        copy.wait_send()
    for copy in stores:
        copy.wait()


def finish(*refs):
    ins, outs, held = refs[:4], refs[4:8], refs[8:12]
    sem_in, sem_out = refs[12:]
    parts = [(n, pl.ds(BLK * k, BLK)) for k, n in enumerate((0, 0, 0))] + [(1, None), (2, None), (3, None)]

    def view(ref, rows):
        return ref if rows is None else ref.at[0, rows, :]

    fetch, store = [], []
    for k, (n, rows) in enumerate(parts):
        here = view(held[n], rows)
        fetch.append(pltpu.make_async_copy(view(ins[n], rows), here, sem_in.at[k]))
        store.append(pltpu.make_async_copy(here, view(outs[n], rows), sem_out.at[k]))
    for copy in fetch:
        copy.start()
    for first, second in zip(fetch, store):
        first.wait()
        second.start()
    for copy in store:
        copy.wait()


def local(queries, key_rows, value_rows, upstream, head_gate, slot_heads):
    hbm = pl.BlockSpec(memory_space=pl.ANY)
    dma = pltpu.SemaphoreType.DMA
    out_shape = (
        jax.ShapeDtypeStruct(queries.shape, BF16),
        jax.ShapeDtypeStruct(key_rows.shape, BF16),
        jax.ShapeDtypeStruct(value_rows.shape, BF16),
        jax.ShapeDtypeStruct(head_gate.shape, F32),
    )
    half = KV_COLS // 2
    rows_of_pair = pltpu.VMEM((PAIRS, SEQ, 128), BF16)
    results = pl.pallas_call(
        kernel,
        out_shape=out_shape,
        in_specs=[hbm] * 6,
        out_specs=(hbm,) * 4,
        scratch_shapes=[
            pltpu.SMEM(slot_heads.shape, jnp.int32),
            pltpu.SMEM(head_gate.shape, F32),
            pltpu.VMEM(key_rows.shape, BF16),
            pltpu.VMEM(value_rows.shape, BF16),
            pltpu.VMEM(key_rows.shape, BF16),
            pltpu.VMEM(value_rows.shape, BF16),
            pltpu.SMEM(head_gate.shape, F32),
            dma((4,)), dma((3,)),
            pltpu.VMEM((2, 4, 2, 4, CHIP, half), BF16),
            pltpu.VMEM((SEQ, KV_COLS), BF16),
            pltpu.VMEM((Q_COLS, KV_COLS), BF16),
            rows_of_pair, rows_of_pair,
            pltpu.VMEM((PAIRS, 128, SEQ), BF16),
            rows_of_pair, rows_of_pair, rows_of_pair, rows_of_pair, rows_of_pair, rows_of_pair,
            pltpu.VMEM((HEADS, SEQ, SEQ), BF16),
            pltpu.VMEM((HEADS, SEQ, SEQ), F32),
            pltpu.VMEM((HEADS, SEQ, SEQ), BF16),
            pltpu.VMEM((HEADS, 8, SEQ), F32),
            pltpu.VMEM((HEADS, 8, SEQ), F32),
            pltpu.VMEM((2, 8, 128), F32),
            pltpu.VMEM((2, 3, 8, 128), F32),
            pltpu.VMEM((2, 4, 2, 4, CHIP, half), BF16),
            pltpu.VMEM((2, 4, 4, CHIP, half), BF16),
            pltpu.VMEM((2, 4, 4, CHIP, half), BF16),
            pltpu.VMEM((2, 4, 4, CHIP, half), BF16),
            pltpu.VMEM((2, 4, CHIP, half), BF16),
            pltpu.VMEM((2, 4, CHIP, half), BF16),
            pltpu.VMEM((4, CHIP, half), BF16),
            pltpu.VMEM((CHIP, half), BF16),
            pltpu.VMEM((4, CHIP, half), BF16),
            dma((2, PAIRS)), dma((NBLK, PAIRS)),
            dma((2, 3)), dma((2, 4)), dma((2, 4, 3)), dma((2, 4, 4)), dma((2, 4)), dma((2, 4)),
            dma((2, 4)), dma((2, 4)), dma((2, 4)), dma((2, 4)), dma((2, 3)), dma((2, 4)),
            dma((2, 3)), dma((2, 3)), dma((3,)), dma((4,)), dma((1,)), dma((4,)),
            pltpu.SemaphoreType.REGULAR((3,)),
        ],
        compiler_params=pltpu.CompilerParams(
            collective_id=0, has_side_effects=True, vmem_limit_bytes=58 * 1024 * 1024
        ),
        name="attention_backward",
    )(slot_heads, head_gate, queries, upstream, key_rows, value_rows)
    return pl.pallas_call(
        finish,
        out_shape=out_shape,
        in_specs=[hbm] * 4,
        out_specs=(hbm,) * 4,
        scratch_shapes=[
            pltpu.VMEM(queries.shape, BF16),
            pltpu.VMEM(key_rows.shape, BF16),
            pltpu.VMEM(value_rows.shape, BF16),
            pltpu.SMEM(head_gate.shape, F32),
            dma((6,)), dma((6,)),
        ],
        name="copy_out",
    )(*results)


def solution(mesh):
    in_specs = (
        P("dp", None, "head"),
        P("dp", "head", None),
        P("dp", "head", None),
        P("dp", None, "head"),
        P("head"),
        P("head"),
    )
    out_specs = (P("dp", None, "head"), P("dp", "head", None), P("dp", "head", None), P("head"))
    return jax.shard_map(local, mesh=mesh, in_specs=in_specs, out_specs=out_specs, check_vma=False)
```
